32 devices in a mesh: tm: 8 (over z, x), chan: 4 (over y, core).
Axes of the slice: x: 2, y: 2, z: 4, core: 2. Of those that a mesh axis runs over, the one named last changes fastest.
Arguments:
- features: bfloat16 [16384, 1024], P('tm', 'chan'), may hold values from -18 to 18
- rec_start: int32 [16384], P('tm'), may hold values from 0 to 16383, as said below
- rec_end: int32 [16384], P('tm'), may hold values from 1 to 16384, as said below
- w_value: bfloat16 [1024, 1024], P(None, 'chan'), may hold values from -0.1875 to 0.1875
- w_gate: bfloat16 [1024, 1024], P(None, 'chan'), may hold values from -0.1875 to 0.1875
- depth_kernel: bfloat16 [9, 1024], P(None, 'chan'), may hold values from -2 to 2
- norm_gain: bfloat16 [1024], P('chan'), may hold values from 0.099609375 to 1.8984375
- norm_shift: bfloat16 [1024], P('chan'), may hold values from -3 to 3
- w_down: bfloat16 [1024, 1024], P('chan'), may hold values from -0.1875 to 0.1875
Outputs:
- mixed: bfloat16 [16384, 1024], P('tm', 'chan')
The draws below stay inside these ranges and needn't reach their ends.
Inputs may be any that keep to these rules, and one draw needn't show every extreme that they name: Frames are packed recordings in order: rec_start[t] <= t < rec_end[t], all frames of a recording share both values, and a recording ends where the next starts. Frame 0 is a recording of its own, and so is the last frame. `rec_end`: as for rec_start.
All inputs are finite; a program needn't handle non-finite values.
Results may differ from the reference program's by a relative error of at most 0.012.
Values may be sent and summed in bfloat16 or wider, within the bound.
A program may use at most 64 MiB of HBM per device.

```python
import jax
import jax.numpy as jnp
from jax import lax

D = 1024
C = 1024
KERNEL = 9
FRAMES = 16384


def segment_law(key):
    base = jax.random.fold_in(key, 11)
    first, second, third = jax.random.split(base, 3)
    index = jnp.arange(FRAMES, dtype=jnp.int32)
    fine_count = (FRAMES + 511) // 512
    coarse_count = (FRAMES + 16383) // 16384
    loud_count = (FRAMES + 4095) // 4096
    fine = jnp.clip(jax.random.normal(first, (fine_count, D), jnp.float32), -3.0, 3.0) * 0.6
    coarse = jnp.clip(jax.random.normal(second, (coarse_count, D), jnp.float32), -3.0, 3.0) * 0.6
    loud = jnp.exp(jax.random.uniform(third, (loud_count,), jnp.float32, -0.3567, 0.3365))
    offset = jnp.take(fine, index // 512, axis=0) + jnp.take(coarse, index // 16384, axis=0)
    loudness = jnp.take(loud, index // 4096, axis=0)
    return (offset, loudness[:, None])


def draw_features(key, part):
    frames = jnp.arange(FRAMES, dtype=jnp.float32)
    ramp = 1.0 + 2.0 * frames / max(FRAMES - 1, 1)
    offset, loudness = segment_law(key)
    noise = jnp.clip(jax.random.normal(key, (FRAMES, D), jnp.float32), -6.0, 6.0)
    values = (noise + offset) * loudness * (0.8 * ramp[:, None])
    return jnp.clip(values, -18.0, 18.0).astype(jnp.bfloat16)


def recording_bounds(key):
    base = jax.random.fold_in(key, 7)
    index = jnp.arange(FRAMES, dtype=jnp.int32)
    marks = jax.random.randint(base, (FRAMES,), 0, 48) == 0
    marks = marks | (index <= 1) | (index == FRAMES - 1)
    starts = lax.cummax(jnp.where(marks, index, 0), axis=0)
    following = jnp.roll(marks, -1) & (index < FRAMES - 1)
    upcoming = jnp.where(following, index + 1, FRAMES)
    ends = lax.cummin(upcoming, axis=0, reverse=True)
    return (starts.astype(jnp.int32), ends.astype(jnp.int32))


def draw_rec_start(key, part):
    return recording_bounds(key)[0]


def draw_rec_end(key, part):
    return recording_bounds(key)[1]


def steps_of(rng, shape, cuts, low, top_value):
    def one(dim, parts):
        heights = jax.random.uniform(jax.random.fold_in(jax.random.fold_in(rng, 6), dim), (parts,), jnp.float32, low / len(cuts), top_value / len(cuts))
        return jnp.repeat(jnp.exp(heights), shape[dim] // parts).reshape((-1,) + (1,) * (len(shape) - dim - 1))

    level = one(*cuts[0])
    for cut in cuts[1:]:
        level = level * one(*cut)
    return level


def normal_values(stream_key, extent, width, reach, cuts=(), kind=jnp.bfloat16):
    entries = width * jax.random.normal(stream_key, extent, jnp.float32)
    if cuts:
        entries = entries * steps_of(stream_key, extent, cuts, -0.22, 0.18)
    return jnp.clip(entries, -reach, reach).astype(kind)


def setup_inputs(seed: int = 0) -> dict:
    key_of = jax.random.split(jax.random.key(seed), 10)
    features = draw_features(jax.random.fold_in(key_of[9], 71), 0)
    rec_start = draw_rec_start(jax.random.fold_in(key_of[9], 71), 0)
    rec_end = draw_rec_end(jax.random.fold_in(key_of[9], 71), 0)
    w_value = normal_values(key_of[3], (D, C), D ** -0.5, 0.1875, ((1, 4),))
    w_gate = normal_values(key_of[4], (D, C), D ** -0.5, 0.1875, ((1, 4),))
    depth_kernel = normal_values(key_of[5], (KERNEL, C), KERNEL ** -0.5, 2.0, ((1, 4),))
    norm_gain = jnp.clip(1.0 + 0.18 * jax.random.normal(key_of[6], (C,), jnp.float32), 0.099609375, 1.8984375).astype(jnp.bfloat16)
    norm_shift = normal_values(key_of[7], (C,), 0.5, 3.0, ((0, 4),))
    w_down = normal_values(key_of[8], (C, D), C ** -0.5, 0.1875, ((0, 4),))
    return dict(features=features, rec_start=rec_start, rec_end=rec_end, w_value=w_value, w_gate=w_gate, depth_kernel=depth_kernel, norm_gain=norm_gain, norm_shift=norm_shift, w_down=w_down)


def reference(features, rec_start, rec_end, w_value, w_gate, depth_kernel, norm_gain, norm_shift, w_down):
    value = jnp.dot(features, w_value, preferred_element_type=jnp.float32)
    gate = jnp.dot(features, w_gate, preferred_element_type=jnp.float32)
    glu = (value * jax.nn.sigmoid(gate)).astype(jnp.bfloat16)
    half = KERNEL // 2
    padded = jnp.pad(glu, ((half, half), (0, 0)))
    frames = jnp.arange(FRAMES, dtype=jnp.int32)
    conv = jnp.zeros((FRAMES, C), jnp.float32)
    for tap in range(KERNEL):
        source = frames + (tap - half)
        usable = (source >= rec_start) & (source < rec_end)
        term = padded[tap:tap + FRAMES].astype(jnp.float32) * depth_kernel[tap].astype(jnp.float32)
        conv = conv + jnp.where(usable[:, None], term, jnp.float32(0.0))
    mean = lax.optimization_barrier(jnp.sum(conv, axis=0)) / FRAMES
    centred = conv - mean
    var = lax.optimization_barrier(jnp.sum(centred * centred, axis=0)) / FRAMES
    normed = centred / jnp.sqrt(var + 1e-05) * norm_gain.astype(jnp.float32) + norm_shift.astype(jnp.float32)
    swished = (normed * jax.nn.sigmoid(normed)).astype(jnp.bfloat16)
    return jnp.dot(swished, w_down, preferred_element_type=jnp.float32).astype(jnp.bfloat16)
```

```python
import functools

import jax
import jax.numpy as jnp
from jax import lax
from jax.experimental import pallas as pl
from jax.experimental.pallas import tpu as pltpu
from jax.sharding import PartitionSpec as P

F32, BF16 = jnp.float32, jnp.bfloat16
GROUP = 4
PARTS = 4
STEPS = 8
PAD = 8
BLOCK = 64
LANES = 128


def swish_gate(value, gate):
    return value * (0.5 * jnp.tanh(0.5 * gate) + 0.5)


def kernel(
    n_tm,
    feat, starts, ends, wv, wg, taps, gain, shift, wdown,
    out,
    xg, wo, wd, par, back, fwd, glu, conv, stat, norm, sw, ob,
    loc, wy_s, wy_r, wf_s, wf_r, par_s, par_r, fc_s, fc_r, fy_s, fy_r, ff_s, ff_r,
    ha_s, ha_r, wd_s, wd_r, st_s, st_r, sw_s, sw_r, oy_s, oy_r,
):
    depth, width = wv.shape
    rows = feat.shape[0] // 2
    part, step_rows = rows // PARTS, rows // STEPS
    piece = depth // GROUP
    n_tap = taps.shape[0]
    reach = n_tap // 2
    n_blocks = 2 * n_tm
    total = n_blocks * rows

    t, chan = lax.axis_index("tm"), lax.axis_index("chan")
    y, core = chan // 2, chan % 2
    oy = 1 - y
    me = 2 * t + y
    across = (t, 2 * oy + core)
    beside = (t, 2 * y + 1 - core)
    diag = (t, 2 * oy + 1 - core)
    group, g = t - t % GROUP, t % GROUP

    def at_block(b):
        return (b // 2, 2 * (b % 2) + core)

    def send(src, dst, s, r, to):
        return pltpu.make_async_remote_copy(
            src_ref=src, dst_ref=dst, send_sem=s, recv_sem=r,
            device_id=to, device_id_type=pl.DeviceIdType.MESH,
        )

    def landed(ref, sem):
        pltpu.make_async_copy(ref, ref, sem).wait()

    barrier = pltpu.get_barrier_semaphore()

    def greet(i, c):
        pl.semaphore_signal(
            barrier, inc=1, device_id=at_block((me + i) % n_blocks),
            device_id_type=pl.DeviceIdType.MESH,
        )
        return c

    lax.fori_loop(1, n_blocks, greet, 0)
    for other in (beside, diag):
        pl.semaphore_signal(
            barrier, inc=1, device_id=other, device_id_type=pl.DeviceIdType.MESH
        )
    pl.semaphore_wait(barrier, n_blocks + 1)

    mine = pl.ds(pl.multiple_of(g * piece, piece), piece)
    cross = [
        send(w.at[mine], wo.at[k, mine], wy_s.at[k], wy_r.at[k], across)
        for k, w in enumerate((wv, wg))
    ]
    for copy in cross:
        copy.start()

    def own_rows(i):
        return pl.ds(pl.multiple_of(y * rows + i * part, part), part)

    def other_rows(i):
        return pl.ds(pl.multiple_of(oy * rows + i * part, part), part)

    def part_rows(i):
        return pl.ds(pl.multiple_of(i * part, part), part)

    def order(i):
        return (3 * i) % PARTS

    def feat_beside(i):
        return send(
            feat.at[own_rows(i)], xg.at[chan, part_rows(i)], fc_s.at[i], fc_r.at[i], beside
        )

    def feat_across(i):
        return send(
            feat.at[other_rows(i)], xg.at[chan, part_rows(i)], fy_s.at[i], fy_r.at[i], across
        )

    def feat_forward(i):
        slot = 2 * oy + core
        return send(
            xg.at[slot, part_rows(i)], xg.at[slot, part_rows(i)], ff_s.at[i], ff_r.at[i], beside
        )

    keep = pltpu.make_async_copy(
        feat.at[pl.ds(pl.multiple_of(y * rows, rows), rows)], xg.at[chan], loc.at[0]
    )
    keep.start()
    for i in range(PARTS):
        feat_beside(order(i)).start()

    for q in range(2):
        lanes = slice(q * LANES, (q + 1) * LANES)
        par[2 * y + q] = jnp.zeros(par.shape[1:], F32)
        par[2 * y + q, 0:n_tap, :] = taps[:, lanes].astype(F32)
        par[2 * y + q, n_tap : n_tap + 1, :] = gain[:, lanes].astype(F32)
        par[2 * y + q, n_tap + 1 : n_tap + 2, :] = shift[:, lanes].astype(F32)
    my_par = par.at[pl.ds(2 * y, 2)]
    par_copy = send(my_par, my_par, par_s, par_r, across)
    par_copy.start()

    groups = rows // LANES
    base = t * 2 * rows + y * rows
    span = pl.ds(pl.multiple_of(y * groups, groups), groups)
    frame = (
        base
        + lax.broadcasted_iota(jnp.int32, (groups, LANES), 0) * LANES
        + lax.broadcasted_iota(jnp.int32, (groups, LANES), 1)
    )
    before = jnp.minimum(frame - starts[span, :], reach).astype(F32)
    after = jnp.minimum(ends[span, :] - 1 - frame, reach).astype(F32)
    for r in range(groups):
        tile = slice(r * LANES, (r + 1) * LANES)
        back[tile, :] = jnp.broadcast_to(before[r : r + 1, :], (LANES, LANES)).T
        fwd[tile, :] = jnp.broadcast_to(after[r : r + 1, :], (LANES, LANES)).T

    def share(k, i):
        return send(
            wo.at[k, mine], wo.at[k, mine], wf_s.at[k, i], wf_r.at[k, i],
            (group + (g + i) % GROUP, chan),
        )

    for k in range(2):
        cross[k].wait_recv()
        for i in range(1, GROUP):
            share(k, i).start()
        if k == 0:
            feat_across(order(0)).start()
    for i in range(1, PARTS):
        feat_across(order(i)).start()
    keep.wait()

    def gated(i, half, value_w, gate_w):
        x = jnp.concatenate([xg[j, part_rows(i), :] for j in range(4)], axis=1)
        value = jnp.dot(x, value_w, preferred_element_type=F32)
        gate = jnp.dot(x, gate_w, preferred_element_type=F32)
        both = swish_gate(value, gate).astype(BF16).astype(F32)
        to = pl.ds(pl.multiple_of(PAD + i * part, PAD), part)
        glu[2 * half, to, :] = both[:, :LANES]
        glu[2 * half + 1, to, :] = both[:, LANES:]

    def first_half(n, c):
        i = order(n)
        feat_across(i).wait_recv()
        feat_forward(i).start()
        feat_beside(i).wait_recv()
        feat_forward(i).wait_recv()
        gated(i, y, wv[...], wg[...])
        return c

    lax.fori_loop(0, PARTS, first_half, 0)

    def down_copy(p, h):
        to = (beside, across, diag)[p]
        to_core = to[1] % 2
        cols = pl.ds(pl.multiple_of((2 * h + to_core) * width, width), width)
        held = pl.ds(pl.multiple_of(chan * width, width), width)
        return send(
            wdown.at[:, cols], wd.at[h, held], wd_s.at[p, h], wd_r.at[p, h], to
        )

    for h in range(2):
        cols = pl.ds(pl.multiple_of((2 * h + core) * width, width), width)
        held = pl.ds(pl.multiple_of(chan * width, width), width)
        pltpu.make_async_copy(wdown.at[:, cols], wd.at[h, held], loc.at[1 + h]).start()

    for k in range(2):
        for i in range(1, GROUP):
            share(k, i).wait_recv()

    def second_half(n, c):
        gated(order(n), oy, wo[0], wo[1])
        return c

    lax.fori_loop(0, 2, second_half, 0)
    right = send(
        glu.at[:, pl.ds(rows, PAD)], glu.at[:, pl.ds(0, PAD)], ha_s.at[0], ha_r.at[0],
        at_block((me + 1) % n_blocks),
    )
    left = send(
        glu.at[:, pl.ds(PAD, PAD)], glu.at[:, pl.ds(rows + PAD, PAD)], ha_s.at[1], ha_r.at[1],
        at_block((me + n_blocks - 1) % n_blocks),
    )
    right.start()
    left.start()
    for p in range(3):
        for h in range(2):
            down_copy(p, h).start()
    lax.fori_loop(2, PARTS, second_half, 0)
    par_copy.wait_recv()

    def convolve(q, b):
        at = pl.multiple_of(b * BLOCK, BLOCK)
        room_back, room_fwd = back[pl.ds(at, BLOCK), :], fwd[pl.ds(at, BLOCK), :]
        acc = jnp.zeros((BLOCK, LANES), F32)
        for k in range(n_tap):
            d = k - reach
            term = glu[q, pl.ds(at + (PAD + d), BLOCK), :] * par[q, k : k + 1, :]
            if d < 0:
                term = jnp.where(room_back >= float(-d), term, 0.0)
            elif d > 0:
                term = jnp.where(room_fwd >= float(d), term, 0.0)
            acc = acc + term
        conv[q, pl.ds(at, BLOCK), :] = acc

    n_inner = rows // BLOCK

    def inner(b, c):
        for q in range(4):
            convolve(q, b)
        return c

    lax.fori_loop(1, n_inner - 1, inner, 0)
    right.wait_recv()
    left.wait_recv()
    inner(0, 0)
    inner(n_inner - 1, 0)

    for q in range(4):
        block = conv[q]
        total_q = jnp.sum(block, axis=0, keepdims=True)
        off = block - total_q * (1.0 / rows)
        stat[me, q : q + 1, :] = total_q
        stat[me, 4 + q : 5 + q, :] = jnp.sum(off * off, axis=0, keepdims=True)

    def tell(i, c):
        send(stat.at[me], stat.at[me], st_s, st_r, at_block((me + i) % n_blocks)).start()
        return c

    lax.fori_loop(1, n_blocks, tell, 0)
    landed(stat.at[pl.ds(0, n_blocks - 1)], st_r)
    sums, squares = stat[:, 0:4, :], stat[:, 4:8, :]
    mean = jnp.sum(sums, axis=0) * (1.0 / total)
    drift = sums * (1.0 / rows) - mean[None]
    var = jnp.sum(squares + float(rows) * (drift * drift), axis=0) * (1.0 / total)
    norm[0:4, :] = mean
    norm[4:8, :] = 1.0 / jnp.sqrt(var + 1e-05)

    def step_at(c):
        return pl.ds(pl.multiple_of(c * step_rows, step_rows), step_rows)

    def pass_on(c):
        mid = sw.at[core, :, step_at(c)]
        return send(mid, mid, sw_s.at[c], sw_r.at[c], beside)

    def activate(c):
        for q in range(4):
            scale = norm[4 + q : 5 + q, :] * par[q, n_tap : n_tap + 1, :]
            x = (conv[q, step_at(c), :] - norm[q : q + 1, :]) * scale
            x = x + par[q, n_tap + 1 : n_tap + 2, :]
            lanes = slice((q % 2) * LANES, (q % 2 + 1) * LANES)
            sw[core, q // 2, step_at(c), lanes] = swish_gate(x, x).astype(BF16)
        pass_on(c).start()

    def home_rows(c):
        return pl.ds(pl.multiple_of(y * rows + c * step_rows, step_rows), step_rows)

    def give(c):
        return send(ob.at[step_at(c)], out.at[home_rows(c)], oy_s.at[c], oy_r.at[c], across)

    def project(c):
        pass_on(c).wait_recv()
        x = jnp.concatenate([sw[j % 2, j // 2, step_at(c), :] for j in range(4)], axis=1)
        ob[step_at(c), :] = jnp.dot(x, wd[oy], preferred_element_type=F32).astype(BF16)
        give(c).start()
        out[home_rows(c), :] = jnp.dot(x, wd[y], preferred_element_type=F32).astype(BF16)

    activate(0)
    for h in range(2):
        held = pl.ds(pl.multiple_of(chan * width, width), width)
        pltpu.make_async_copy(
            wdown.at[:, pl.ds(0, width)], wd.at[h, held], loc.at[1 + h]
        ).wait()
        for p in range(3):
            down_copy(p, h).wait_recv()

    def advance(c, carry):
        activate(c + 1)
        project(c)
        return carry

    lax.fori_loop(0, STEPS - 1, advance, 0)
    project(STEPS - 1)

    for copy in cross:
        copy.wait_send()
    par_copy.wait_send()
    right.wait_send()
    left.wait_send()
    for k in range(2):
        for i in range(1, GROUP):
            share(k, i).wait_send()
    for p in range(3):
        for h in range(2):
            down_copy(p, h).wait_send()
    landed(stat.at[pl.ds(0, n_blocks - 1)], st_s)

    def drain(i, c):
        feat_beside(i).wait_send()
        feat_across(i).wait_send()
        feat_forward(i).wait_send()
        return c

    lax.fori_loop(0, PARTS, drain, 0)

    def finish(c, carry):
        pass_on(c).wait_send()
        give(c).wait()
        return carry

    lax.fori_loop(0, STEPS, finish, 0)


def body(
    n_tm,
    features, rec_start, rec_end, w_value, w_gate, depth_kernel, norm_gain, norm_shift, w_down,
):
    frames, width = features.shape
    depth = w_value.shape[0]
    rows = frames // 2
    dma = pltpu.SemaphoreType.DMA
    vmem = pl.BlockSpec(memory_space=pltpu.VMEM)
    n_blocks = 2 * n_tm
    return pl.pallas_call(
        functools.partial(kernel, n_tm),
        out_shape=jax.ShapeDtypeStruct((frames, width), BF16),
        in_specs=[vmem] * 9,
        out_specs=vmem,
        scratch_shapes=[
            pltpu.VMEM((4, rows, width), BF16),
            pltpu.VMEM((2, depth, width), BF16),
            pltpu.VMEM((2, 4 * width, width), BF16),
            pltpu.VMEM((4, 16, LANES), F32),
            pltpu.VMEM((rows, LANES), F32),
            pltpu.VMEM((rows, LANES), F32),
            pltpu.VMEM((4, rows + 2 * PAD, LANES), F32),
            pltpu.VMEM((4, rows, LANES), F32),
            pltpu.VMEM((n_blocks, 8, LANES), F32),
            pltpu.VMEM((8, LANES), F32),
            pltpu.VMEM((2, 2, rows, width), BF16),
            pltpu.VMEM((rows, width), BF16),
            dma((3,)),
            dma((2,)), dma((2,)),
            dma((2, GROUP)), dma((2, GROUP)),
            dma, dma,
            dma((PARTS,)), dma((PARTS,)),
            dma((PARTS,)), dma((PARTS,)),
            dma((PARTS,)), dma((PARTS,)),
            dma((2,)), dma((2,)),
            dma((3, 2)), dma((3, 2)),
            dma, dma,
            dma((STEPS,)), dma((STEPS,)),
            dma((STEPS,)), dma((STEPS,)),
        ],
        compiler_params=pltpu.CompilerParams(
            collective_id=0, has_side_effects=True, vmem_limit_bytes=40 * 1024 * 1024
        ),
    )(
        features,
        rec_start.reshape(-1, LANES),
        rec_end.reshape(-1, LANES),
        w_value,
        w_gate,
        depth_kernel,
        norm_gain.reshape(1, -1),
        norm_shift.reshape(1, -1),
        w_down,
    )


def solution(mesh):
    in_specs = (
        P("tm", "chan"),
        P("tm"),
        P("tm"),
        P(None, "chan"),
        P(None, "chan"),
        P(None, "chan"),
        P("chan"),
        P("chan"),
        P("chan", None),
    )
    return jax.shard_map(
        functools.partial(body, mesh.shape["tm"]),
        mesh=mesh,
        in_specs=in_specs,
        out_specs=P("tm", "chan"),
        check_vma=False,
    )
```

```python
import functools

import jax
import jax.numpy as jnp
from jax import lax
from jax.experimental import pallas as pl
from jax.experimental.pallas import tpu as pltpu
from jax.sharding import PartitionSpec as P

F32, BF16 = jnp.float32, jnp.bfloat16
GROUP = 4
PARTS = 4
STEPS = 8
PAD = 8
BLOCK = 64
LANES = 128


def swish_gate(value, gate):
    return value * (0.5 * jnp.tanh(0.5 * gate) + 0.5)


def kernel(
    n_tm,
    feat, starts_in, ends_in, wv_in, wg_in, taps_in, gain_in, shift_in, wdown,
    out,
    wv, wg, starts, ends, taps, gain, shift,
    xg, wo, wd, par, back, fwd, glu, conv, stat, norm, sw, ob,
    loc, wy_s, wy_r, wf_s, wf_r, par_s, par_r, fc_s, fc_r, fy_s, fy_r, ff_s, ff_r,
    ha_s, ha_r, wd_s, wd_r, st_s, st_r, sw_s, sw_r, oy_s, oy_r,
):
    depth, width = wv.shape
    rows = feat.shape[0] // 2
    part, step_rows = rows // PARTS, rows // STEPS
    piece = depth // GROUP
    n_tap = taps.shape[0]
    reach = n_tap // 2
    n_blocks = 2 * n_tm
    total = n_blocks * rows

    t, chan = lax.axis_index("tm"), lax.axis_index("chan")
    y, core = chan // 2, chan % 2
    oy = 1 - y
    me = 2 * t + y
    across = (t, 2 * oy + core)
    beside = (t, 2 * y + 1 - core)
    diag = (t, 2 * oy + 1 - core)
    group, g = t - t % GROUP, t % GROUP

    def at_block(b):
        return (b // 2, 2 * (b % 2) + core)

    def send(src, dst, s, r, to):
        return pltpu.make_async_remote_copy(
            src_ref=src, dst_ref=dst, send_sem=s, recv_sem=r,
            device_id=to, device_id_type=pl.DeviceIdType.MESH,
        )

    def landed(ref, sem):
        pltpu.make_async_copy(ref, ref, sem).wait()

    keep = pltpu.make_async_copy(
        feat.at[pl.ds(pl.multiple_of(y * rows, rows), rows)], xg.at[chan], loc.at[0]
    )
    loads = [
        pltpu.make_async_copy(src, dst, loc.at[3 + i])
        for i, (src, dst) in enumerate(
            (
                (starts_in, starts),
                (ends_in, ends),
                (taps_in, taps),
                (gain_in, gain),
                (shift_in, shift),
                (wv_in, wv),
                (wg_in, wg),
            )
        )
    ]
    for copy in loads:
        copy.start()
    keep.start()

    barrier = pltpu.get_barrier_semaphore()

    def greet(i, c):
        pl.semaphore_signal(
            barrier, inc=1, device_id=at_block((me + i) % n_blocks),
            device_id_type=pl.DeviceIdType.MESH,
        )
        return c

    lax.fori_loop(1, n_blocks, greet, 0)
    for other in (beside, diag):
        pl.semaphore_signal(
            barrier, inc=1, device_id=other, device_id_type=pl.DeviceIdType.MESH
        )
    pl.semaphore_wait(barrier, n_blocks + 1)

    mine = pl.ds(pl.multiple_of(g * piece, piece), piece)
    cross = [
        send(w.at[mine], wo.at[k, mine], wy_s.at[k], wy_r.at[k], across)
        for k, w in enumerate((wv_in, wg_in))
    ]
    for copy in cross:
        copy.start()

    def own_rows(i):
        return pl.ds(pl.multiple_of(y * rows + i * part, part), part)

    def other_rows(i):
        return pl.ds(pl.multiple_of(oy * rows + i * part, part), part)

    def part_rows(i):
        return pl.ds(pl.multiple_of(i * part, part), part)

    def order(i):
        return (3 * i) % PARTS

    def feat_beside(i):
        return send(
            feat.at[own_rows(i)], xg.at[chan, part_rows(i)], fc_s.at[i], fc_r.at[i], beside
        )

    def feat_across(i):
        return send(
            feat.at[other_rows(i)], xg.at[chan, part_rows(i)], fy_s.at[i], fy_r.at[i], across
        )

    def feat_forward(i):
        slot = 2 * oy + core
        return send(
            xg.at[slot, part_rows(i)], xg.at[slot, part_rows(i)], ff_s.at[i], ff_r.at[i], beside
        )

    for i in range(PARTS):
        feat_beside(order(i)).start()

    for copy in loads[:5]:
        copy.wait()
    gain_row = gain[...].astype(F32).reshape(1, width)
    shift_row = shift[...].astype(F32).reshape(1, width)
    for q in range(2):
        lanes = slice(q * LANES, (q + 1) * LANES)
        par[2 * y + q] = jnp.zeros(par.shape[1:], F32)
        par[2 * y + q, 0:n_tap, :] = taps[:, lanes].astype(F32)
        par[2 * y + q, n_tap : n_tap + 1, :] = gain_row[:, lanes]
        par[2 * y + q, n_tap + 1 : n_tap + 2, :] = shift_row[:, lanes]
    my_par = par.at[pl.ds(2 * y, 2)]
    par_copy = send(my_par, my_par, par_s, par_r, across)
    par_copy.start()

    groups = rows // LANES
    base = t * 2 * rows + y * rows
    span = pl.ds(pl.multiple_of(y * groups, groups), groups)
    frame = (
        base
        + lax.broadcasted_iota(jnp.int32, (groups, LANES), 0) * LANES
        + lax.broadcasted_iota(jnp.int32, (groups, LANES), 1)
    )
    before = jnp.minimum(frame - starts[span, :], reach).astype(F32)
    after = jnp.minimum(ends[span, :] - 1 - frame, reach).astype(F32)
    for r in range(groups):
        tile = slice(r * LANES, (r + 1) * LANES)
        back[tile, :] = jnp.broadcast_to(before[r : r + 1, :], (LANES, LANES)).T
        fwd[tile, :] = jnp.broadcast_to(after[r : r + 1, :], (LANES, LANES)).T

    def share(k, i):
        return send(
            wo.at[k, mine], wo.at[k, mine], wf_s.at[k, i], wf_r.at[k, i],
            (group + (g + i) % GROUP, chan),
        )

    for k in range(2):
        cross[k].wait_recv()
        for i in range(1, GROUP):
            share(k, i).start()
        if k == 0:
            feat_across(order(0)).start()
    for i in range(1, PARTS):
        feat_across(order(i)).start()
    keep.wait()
    for copy in loads[5:]:
        copy.wait()

    def gated(i, half, value_w, gate_w):
        x = jnp.concatenate([xg[j, part_rows(i), :] for j in range(4)], axis=1)
        value = jnp.dot(x, value_w, preferred_element_type=F32)
        gate = jnp.dot(x, gate_w, preferred_element_type=F32)
        both = swish_gate(value, gate).astype(BF16).astype(F32)
        to = pl.ds(pl.multiple_of(PAD + i * part, PAD), part)
        glu[2 * half, to, :] = both[:, :LANES]
        glu[2 * half + 1, to, :] = both[:, LANES:]

    def first_half(n, c):
        i = order(n)
        feat_across(i).wait_recv()
        feat_forward(i).start()
        feat_beside(i).wait_recv()
        feat_forward(i).wait_recv()
        gated(i, y, wv[...], wg[...])
        return c

    lax.fori_loop(0, PARTS, first_half, 0)

    def down_copy(p, h):
        to = (beside, across, diag)[p]
        to_core = to[1] % 2
        cols = pl.ds(pl.multiple_of((2 * h + to_core) * width, width), width)
        held = pl.ds(pl.multiple_of(chan * width, width), width)
        return send(
            wdown.at[:, cols], wd.at[h, held], wd_s.at[p, h], wd_r.at[p, h], to
        )

    for h in range(2):
        cols = pl.ds(pl.multiple_of((2 * h + core) * width, width), width)
        held = pl.ds(pl.multiple_of(chan * width, width), width)
        pltpu.make_async_copy(wdown.at[:, cols], wd.at[h, held], loc.at[1 + h]).start()

    for k in range(2):
        for i in range(1, GROUP):
            share(k, i).wait_recv()

    def second_half(n, c):
        gated(order(n), oy, wo[0], wo[1])
        return c

    lax.fori_loop(0, 2, second_half, 0)
    right = send(
        glu.at[:, pl.ds(rows, PAD)], glu.at[:, pl.ds(0, PAD)], ha_s.at[0], ha_r.at[0],
        at_block((me + 1) % n_blocks),
    )
    left = send(
        glu.at[:, pl.ds(PAD, PAD)], glu.at[:, pl.ds(rows + PAD, PAD)], ha_s.at[1], ha_r.at[1],
        at_block((me + n_blocks - 1) % n_blocks),
    )
    right.start()
    left.start()
    for p in range(3):
        for h in range(2):
            down_copy(p, h).start()
    lax.fori_loop(2, PARTS, second_half, 0)
    par_copy.wait_recv()

    def convolve(q, b):
        at = pl.multiple_of(b * BLOCK, BLOCK)
        room_back, room_fwd = back[pl.ds(at, BLOCK), :], fwd[pl.ds(at, BLOCK), :]
        acc = jnp.zeros((BLOCK, LANES), F32)
        for k in range(n_tap):
            d = k - reach
            term = glu[q, pl.ds(at + (PAD + d), BLOCK), :] * par[q, k : k + 1, :]
            if d < 0:
                term = jnp.where(room_back >= float(-d), term, 0.0)
            elif d > 0:
                term = jnp.where(room_fwd >= float(d), term, 0.0)
            acc = acc + term
        conv[q, pl.ds(at, BLOCK), :] = acc

    n_inner = rows // BLOCK

    def inner(b, c):
        for q in range(4):
            convolve(q, b)
        return c

    lax.fori_loop(1, n_inner - 1, inner, 0)
    right.wait_recv()
    left.wait_recv()
    inner(0, 0)
    inner(n_inner - 1, 0)

    for q in range(4):
        block = conv[q]
        total_q = jnp.sum(block, axis=0, keepdims=True)
        off = block - total_q * (1.0 / rows)
        stat[me, q : q + 1, :] = total_q
        stat[me, 4 + q : 5 + q, :] = jnp.sum(off * off, axis=0, keepdims=True)

    def tell(i, c):
        send(stat.at[me], stat.at[me], st_s, st_r, at_block((me + i) % n_blocks)).start()
        return c

    lax.fori_loop(1, n_blocks, tell, 0)
    landed(stat.at[pl.ds(0, n_blocks - 1)], st_r)
    sums, squares = stat[:, 0:4, :], stat[:, 4:8, :]
    mean = jnp.sum(sums, axis=0) * (1.0 / total)
    drift = sums * (1.0 / rows) - mean[None]
    var = jnp.sum(squares + float(rows) * (drift * drift), axis=0) * (1.0 / total)
    norm[0:4, :] = mean
    norm[4:8, :] = 1.0 / jnp.sqrt(var + 1e-05)

    def step_at(c):
        return pl.ds(pl.multiple_of(c * step_rows, step_rows), step_rows)

    def pass_on(c):
        mid = sw.at[core, :, step_at(c)]
        return send(mid, mid, sw_s.at[c], sw_r.at[c], beside)

    def activate(c):
        for q in range(4):
            scale = norm[4 + q : 5 + q, :] * par[q, n_tap : n_tap + 1, :]
            x = (conv[q, step_at(c), :] - norm[q : q + 1, :]) * scale
            x = x + par[q, n_tap + 1 : n_tap + 2, :]
            lanes = slice((q % 2) * LANES, (q % 2 + 1) * LANES)
            sw[core, q // 2, step_at(c), lanes] = swish_gate(x, x).astype(BF16)
        pass_on(c).start()

    def home_rows(c):
        return pl.ds(pl.multiple_of(y * rows + c * step_rows, step_rows), step_rows)

    def give(c):
        return send(ob.at[step_at(c)], out.at[home_rows(c)], oy_s.at[c], oy_r.at[c], across)

    def project(c):
        pass_on(c).wait_recv()
        x = jnp.concatenate([sw[j % 2, j // 2, step_at(c), :] for j in range(4)], axis=1)
        ob[step_at(c), :] = jnp.dot(x, wd[oy], preferred_element_type=F32).astype(BF16)
        give(c).start()
        out[home_rows(c), :] = jnp.dot(x, wd[y], preferred_element_type=F32).astype(BF16)

    activate(0)
    for h in range(2):
        held = pl.ds(pl.multiple_of(chan * width, width), width)
        pltpu.make_async_copy(
            wdown.at[:, pl.ds(0, width)], wd.at[h, held], loc.at[1 + h]
        ).wait()
        for p in range(3):
            down_copy(p, h).wait_recv()

    def advance(c, carry):
        activate(c + 1)
        project(c)
        return carry

    lax.fori_loop(0, STEPS - 1, advance, 0)
    project(STEPS - 1)

    for copy in cross:
        copy.wait_send()
    par_copy.wait_send()
    right.wait_send()
    left.wait_send()
    for k in range(2):
        for i in range(1, GROUP):
            share(k, i).wait_send()
    for p in range(3):
        for h in range(2):
            down_copy(p, h).wait_send()
    landed(stat.at[pl.ds(0, n_blocks - 1)], st_s)

    def drain(i, c):
        feat_beside(i).wait_send()
        feat_across(i).wait_send()
        feat_forward(i).wait_send()
        return c

    lax.fori_loop(0, PARTS, drain, 0)

    def finish(c, carry):
        pass_on(c).wait_send()
        give(c).wait()
        return carry

    lax.fori_loop(0, STEPS, finish, 0)


def body(
    n_tm,
    features, rec_start, rec_end, w_value, w_gate, depth_kernel, norm_gain, norm_shift, w_down,
):
    frames, width = features.shape
    depth = w_value.shape[0]
    rows = frames // 2
    dma = pltpu.SemaphoreType.DMA
    vmem = pl.BlockSpec(memory_space=pltpu.VMEM)
    n_blocks = 2 * n_tm
    return pl.pallas_call(
        functools.partial(kernel, n_tm),
        out_shape=jax.ShapeDtypeStruct((frames, width), BF16),
        in_specs=[pl.BlockSpec(memory_space=pltpu.HBM)] * 9,
        out_specs=vmem,
        scratch_shapes=[
            pltpu.VMEM((depth, width), BF16),
            pltpu.VMEM((depth, width), BF16),
            pltpu.VMEM((frames // LANES, LANES), jnp.int32),
            pltpu.VMEM((frames // LANES, LANES), jnp.int32),
            pltpu.VMEM(depth_kernel.shape, BF16),
            pltpu.VMEM((width,), BF16),
            pltpu.VMEM((width,), BF16),
            pltpu.VMEM((4, rows, width), BF16),
            pltpu.VMEM((2, depth, width), BF16),
            pltpu.VMEM((2, 4 * width, width), BF16),
            pltpu.VMEM((4, 16, LANES), F32),
            pltpu.VMEM((rows, LANES), F32),
            pltpu.VMEM((rows, LANES), F32),
            pltpu.VMEM((4, rows + 2 * PAD, LANES), F32),
            pltpu.VMEM((4, rows, LANES), F32),
            pltpu.VMEM((n_blocks, 8, LANES), F32),
            pltpu.VMEM((8, LANES), F32),
            pltpu.VMEM((2, 2, rows, width), BF16),
            pltpu.VMEM((rows, width), BF16),
            dma((10,)),
            dma((2,)), dma((2,)),
            dma((2, GROUP)), dma((2, GROUP)),
            dma, dma,
            dma((PARTS,)), dma((PARTS,)),
            dma((PARTS,)), dma((PARTS,)),
            dma((PARTS,)), dma((PARTS,)),
            dma((2,)), dma((2,)),
            dma((3, 2)), dma((3, 2)),
            dma, dma,
            dma((STEPS,)), dma((STEPS,)),
            dma((STEPS,)), dma((STEPS,)),
        ],
        compiler_params=pltpu.CompilerParams(
            collective_id=0, has_side_effects=True, vmem_limit_bytes=62 * 1024 * 1024
        ),
    )(
        features,
        rec_start.reshape(-1, LANES),
        rec_end.reshape(-1, LANES),
        w_value,
        w_gate,
        depth_kernel,
        norm_gain,
        norm_shift,
        w_down,
    )


def solution(mesh):
    in_specs = (
        P("tm", "chan"),
        P("tm"),
        P("tm"),
        P(None, "chan"),
        P(None, "chan"),
        P(None, "chan"),
        P("chan"),
        P("chan"),
        P("chan", None),
    )
    return jax.shard_map(
        functools.partial(body, mesh.shape["tm"]),
        mesh=mesh,
        in_specs=in_specs,
        out_specs=P("tm", "chan"),
        check_vma=False,
    )
```

```python
import functools

import jax
import jax.numpy as jnp
from jax import lax
from jax.experimental import pallas as pl
from jax.experimental.pallas import tpu as pltpu
from jax.sharding import PartitionSpec as P

F32, BF16 = jnp.float32, jnp.bfloat16
GROUP = 4
PARTS = 4
STEPS = 8
PAD = 8
BLOCK = 64
LANES = 128


def swish_gate(value, gate):
    return value * (0.5 * jnp.tanh(0.5 * gate) + 0.5)


def kernel(
    n_tm,
    feat, starts_in, ends_in, wv_in, wg_in, taps_in, gain_in, shift_in, wdown,
    out,
    wv, wg, starts, ends, taps, gain, shift,
    xg, wo, wd, wdx, par, back, fwd, glu, conv, stat, norm, sw, ob,
    loc, wy_s, wy_r, wf_s, wf_r, par_s, par_r, fc_s, fc_r, fy_s, fy_r, ff_s, ff_r,
    ha_s, ha_r, wx_s, wx_r, wb_s, wb_r, wd_s, wd_r, st_s, st_r, sw_s, sw_r, oy_s, oy_r,
):
    depth, width = wv.shape
    rows = feat.shape[0] // 2
    part, step_rows = rows // PARTS, rows // STEPS
    piece = depth // GROUP
    n_tap = taps.shape[0]
    reach = n_tap // 2
    n_blocks = 2 * n_tm
    total = n_blocks * rows

    t, chan = lax.axis_index("tm"), lax.axis_index("chan")
    y, core = chan // 2, chan % 2
    oy = 1 - y
    me = 2 * t + y
    across = (t, 2 * oy + core)
    beside = (t, 2 * y + 1 - core)
    group, g = t - t % GROUP, t % GROUP

    def at_block(b):
        return (b // 2, 2 * (b % 2) + core)

    def send(src, dst, s, r, to):
        return pltpu.make_async_remote_copy(
            src_ref=src, dst_ref=dst, send_sem=s, recv_sem=r,
            device_id=to, device_id_type=pl.DeviceIdType.MESH,
        )

    def landed(ref, sem):
        pltpu.make_async_copy(ref, ref, sem).wait()

    keep = pltpu.make_async_copy(
        feat.at[pl.ds(pl.multiple_of(y * rows, rows), rows)], xg.at[chan], loc.at[0]
    )
    loads = [
        pltpu.make_async_copy(src, dst, loc.at[3 + i])
        for i, (src, dst) in enumerate(
            (
                (starts_in, starts),
                (ends_in, ends),
                (taps_in, taps),
                (gain_in, gain),
                (shift_in, shift),
                (wv_in, wv),
                (wg_in, wg),
            )
        )
    ]
    for copy in loads:
        copy.start()
    keep.start()

    barrier = pltpu.get_barrier_semaphore()

    def greet(i, c):
        pl.semaphore_signal(
            barrier, inc=1, device_id=at_block((me + i) % n_blocks),
            device_id_type=pl.DeviceIdType.MESH,
        )
        return c

    lax.fori_loop(1, n_blocks, greet, 0)
    for i in range(GROUP):
        pl.semaphore_signal(
            barrier, inc=1, device_id=(group + (g + i) % GROUP, beside[1]),
            device_id_type=pl.DeviceIdType.MESH,
        )
    pl.semaphore_wait(barrier, n_blocks - 1 + GROUP)

    mine = pl.ds(pl.multiple_of(g * piece, piece), piece)
    cross = [
        send(w.at[mine], wo.at[k, mine], wy_s.at[k], wy_r.at[k], across)
        for k, w in enumerate((wv_in, wg_in))
    ]
    for copy in cross:
        copy.start()

    def own_rows(i):
        return pl.ds(pl.multiple_of(y * rows + i * part, part), part)

    def other_rows(i):
        return pl.ds(pl.multiple_of(oy * rows + i * part, part), part)

    def part_rows(i):
        return pl.ds(pl.multiple_of(i * part, part), part)

    def order(i):
        return (3 * i) % PARTS

    def feat_beside(i):
        return send(
            feat.at[own_rows(i)], xg.at[chan, part_rows(i)], fc_s.at[i], fc_r.at[i], beside
        )

    def feat_across(i):
        return send(
            feat.at[other_rows(i)], xg.at[chan, part_rows(i)], fy_s.at[i], fy_r.at[i], across
        )

    def feat_forward(i):
        slot = 2 * oy + core
        return send(
            xg.at[slot, part_rows(i)], xg.at[slot, part_rows(i)], ff_s.at[i], ff_r.at[i], beside
        )

    for i in range(PARTS):
        feat_beside(order(i)).start()

    for copy in loads[:5]:
        copy.wait()
    gain_row = gain[...].astype(F32).reshape(1, width)
    shift_row = shift[...].astype(F32).reshape(1, width)
    for q in range(2):
        lanes = slice(q * LANES, (q + 1) * LANES)
        par[2 * y + q] = jnp.zeros(par.shape[1:], F32)
        par[2 * y + q, 0:n_tap, :] = taps[:, lanes].astype(F32)
        par[2 * y + q, n_tap : n_tap + 1, :] = gain_row[:, lanes]
        par[2 * y + q, n_tap + 1 : n_tap + 2, :] = shift_row[:, lanes]
    my_par = par.at[pl.ds(2 * y, 2)]
    par_copy = send(my_par, my_par, par_s, par_r, across)
    par_copy.start()

    groups = rows // LANES
    base = t * 2 * rows + y * rows
    span = pl.ds(pl.multiple_of(y * groups, groups), groups)
    frame = (
        base
        + lax.broadcasted_iota(jnp.int32, (groups, LANES), 0) * LANES
        + lax.broadcasted_iota(jnp.int32, (groups, LANES), 1)
    )
    before = jnp.minimum(frame - starts[span, :], reach).astype(F32)
    after = jnp.minimum(ends[span, :] - 1 - frame, reach).astype(F32)
    for r in range(groups):
        tile = slice(r * LANES, (r + 1) * LANES)
        back[tile, :] = jnp.broadcast_to(before[r : r + 1, :], (LANES, LANES)).T
        fwd[tile, :] = jnp.broadcast_to(after[r : r + 1, :], (LANES, LANES)).T

    def share(k, i):
        return send(
            wo.at[k, mine], wo.at[k, mine], wf_s.at[k, i], wf_r.at[k, i],
            (group + (g + i) % GROUP, chan),
        )

    for k in range(2):
        cross[k].wait_recv()
        for i in range(1, GROUP):
            share(k, i).start()
        if k == 0:
            feat_across(order(0)).start()
    for i in range(1, PARTS):
        feat_across(order(i)).start()
    keep.wait()
    for copy in loads[5:]:
        copy.wait()

    def gated(i, half, value_w, gate_w):
        x = jnp.concatenate([xg[j, part_rows(i), :] for j in range(4)], axis=1)
        value = jnp.dot(x, value_w, preferred_element_type=F32)
        gate = jnp.dot(x, gate_w, preferred_element_type=F32)
        both = swish_gate(value, gate).astype(BF16).astype(F32)
        to = pl.ds(pl.multiple_of(PAD + i * part, PAD), part)
        glu[2 * half, to, :] = both[:, :LANES]
        glu[2 * half + 1, to, :] = both[:, LANES:]

    def first_half(i):
        feat_across(i).wait_recv()
        feat_forward(i).start()
        feat_beside(i).wait_recv()
        feat_forward(i).wait_recv()
        gated(i, y, wv[...], wg[...])

    def second_half(i):
        gated(i, oy, wo[0], wo[1])

    def halos(half):
        pair = pl.ds(2 * half, 2)
        return (
            send(
                glu.at[pair, pl.ds(rows, PAD)], glu.at[pair, pl.ds(0, PAD)],
                ha_s.at[half, 0], ha_r.at[half, 0], at_block((me + 1) % n_blocks),
            ),
            send(
                glu.at[pair, pl.ds(PAD, PAD)], glu.at[pair, pl.ds(rows + PAD, PAD)],
                ha_s.at[half, 1], ha_r.at[half, 1], at_block((me + n_blocks - 1) % n_blocks),
            ),
        )

    down_piece = width // GROUP
    cut = pl.ds(pl.multiple_of(g * down_piece, down_piece), down_piece)
    down_cross = send(wdown.at[cut], wdx, wx_s, wx_r, across)

    def down_cols(h, c):
        return pl.ds(pl.multiple_of((2 * h + c) * width, width), width)

    own_held = pl.ds(pl.multiple_of(chan * width, width), width)

    def down_beside(h):
        return send(
            wdown.at[:, down_cols(h, 1 - core)], wd.at[h, own_held], wb_s.at[h], wb_r.at[h], beside
        )

    def down_keep(h):
        return pltpu.make_async_copy(
            wdown.at[:, down_cols(h, core)], wd.at[h, own_held], loc.at[1 + h]
        )

    def down_share(o, i, h):
        to_core = (core, 1 - core)[o]
        held = pl.ds(
            pl.multiple_of(across[1] * width + g * down_piece, down_piece), down_piece
        )
        src, dst = wdx.at[:, down_cols(h, to_core)], wd.at[h, held]
        if o == 0 and i == 0:
            return pltpu.make_async_copy(src, dst, loc.at[10 + h])
        to = (group + (g + i) % GROUP, 2 * y + to_core)
        return send(src, dst, wd_s.at[o, i, h], wd_r.at[o, i, h], to)

    shares = [
        (o, i, h) for i in (1, 2, 3, 0) for o in range(2) for h in range(2) if (o, i) != (0, 0)
    ]
    kept = [(0, 0, h) for h in range(2)]

    def convolve(q, b):
        at = pl.multiple_of(b * BLOCK, BLOCK)
        room_back, room_fwd = back[pl.ds(at, BLOCK), :], fwd[pl.ds(at, BLOCK), :]
        acc = jnp.zeros((BLOCK, LANES), F32)
        for k in range(n_tap):
            d = k - reach
            term = glu[q, pl.ds(at + (PAD + d), BLOCK), :] * par[q, k : k + 1, :]
            if d < 0:
                term = jnp.where(room_back >= float(-d), term, 0.0)
            elif d > 0:
                term = jnp.where(room_fwd >= float(d), term, 0.0)
            acc = acc + term
        conv[q, pl.ds(at, BLOCK), :] = acc

    last = order(PARTS - 1)
    n_inner = rows // BLOCK
    low, high = last * part // BLOCK - 1, (last + 1) * part // BLOCK + 1

    def inner(half):
        def run(b, c):
            for q in range(2):
                convolve(2 * half + q, b)
            return c

        return run

    first, final = order(0), order(1)
    first_half(first)
    first_half(final)
    for copy in halos(y):
        copy.start()
    for n in range(2, PARTS - 1):
        first_half(order(n))
    for k in range(2):
        for i in range(1, GROUP):
            share(k, i).wait_recv()
    second_half(first)
    second_half(final)
    for copy in halos(oy):
        copy.start()
    down_cross.start()
    for h in range(2):
        down_keep(h).start()
        down_beside(h).start()
    for n in range(2, PARTS - 1):
        second_half(order(n))
    par_copy.wait_recv()
    for half in (y, oy):
        for copy in halos(half):
            copy.wait_recv()
        lax.fori_loop(0, low, inner(half), 0)
        lax.fori_loop(high, n_inner, inner(half), 0)
    down_cross.wait_recv()
    for key in shares + kept:
        down_share(*key).start()
    first_half(last)
    second_half(last)
    for half in (y, oy):
        lax.fori_loop(low, high, inner(half), 0)

    for q in range(4):
        block = conv[q]
        total_q = jnp.sum(block, axis=0, keepdims=True)
        off = block - total_q * (1.0 / rows)
        stat[me, q : q + 1, :] = total_q
        stat[me, 4 + q : 5 + q, :] = jnp.sum(off * off, axis=0, keepdims=True)

    def tell(i, c):
        send(stat.at[me], stat.at[me], st_s, st_r, at_block((me + i) % n_blocks)).start()
        return c

    lax.fori_loop(1, n_blocks, tell, 0)
    landed(stat.at[pl.ds(0, n_blocks - 1)], st_r)
    sums, squares = stat[:, 0:4, :], stat[:, 4:8, :]
    mean = jnp.sum(sums, axis=0) * (1.0 / total)
    drift = sums * (1.0 / rows) - mean[None]
    var = jnp.sum(squares + float(rows) * (drift * drift), axis=0) * (1.0 / total)
    norm[0:4, :] = mean
    norm[4:8, :] = 1.0 / jnp.sqrt(var + 1e-05)

    def step_at(c):
        return pl.ds(pl.multiple_of(c * step_rows, step_rows), step_rows)

    def pass_on(c):
        mid = sw.at[core, :, step_at(c)]
        return send(mid, mid, sw_s.at[c], sw_r.at[c], beside)

    def activate(c):
        for q in range(4):
            scale = norm[4 + q : 5 + q, :] * par[q, n_tap : n_tap + 1, :]
            x = (conv[q, step_at(c), :] - norm[q : q + 1, :]) * scale
            x = x + par[q, n_tap + 1 : n_tap + 2, :]
            lanes = slice((q % 2) * LANES, (q % 2 + 1) * LANES)
            sw[core, q // 2, step_at(c), lanes] = swish_gate(x, x).astype(BF16)
        pass_on(c).start()

    def home_rows(c):
        return pl.ds(pl.multiple_of(y * rows + c * step_rows, step_rows), step_rows)

    def give(c):
        return send(ob.at[step_at(c)], out.at[home_rows(c)], oy_s.at[c], oy_r.at[c], across)

    def project(c):
        pass_on(c).wait_recv()
        x = jnp.concatenate([sw[j % 2, j // 2, step_at(c), :] for j in range(4)], axis=1)
        ob[step_at(c), :] = jnp.dot(x, wd[oy], preferred_element_type=F32).astype(BF16)
        give(c).start()
        out[home_rows(c), :] = jnp.dot(x, wd[y], preferred_element_type=F32).astype(BF16)

    activate(0)
    for h in range(2):
        down_keep(h).wait()
        down_beside(h).wait_recv()
    for key in shares:
        down_share(*key).wait_recv()
    for key in kept:
        down_share(*key).wait()

    def advance(c, carry):
        activate(c + 1)
        project(c)
        return carry

    lax.fori_loop(0, STEPS - 1, advance, 0)
    project(STEPS - 1)

    for copy in cross:
        copy.wait_send()
    par_copy.wait_send()
    for half in (y, oy):
        for copy in halos(half):
            copy.wait_send()
    for k in range(2):
        for i in range(1, GROUP):
            share(k, i).wait_send()
    down_cross.wait_send()
    for h in range(2):
        down_beside(h).wait_send()
    for key in shares:
        down_share(*key).wait_send()
    landed(stat.at[pl.ds(0, n_blocks - 1)], st_s)

    def drain(i, c):
        feat_beside(i).wait_send()
        feat_across(i).wait_send()
        feat_forward(i).wait_send()
        return c

    lax.fori_loop(0, PARTS, drain, 0)

    def finish(c, carry):
        pass_on(c).wait_send()
        give(c).wait()
        return carry

    lax.fori_loop(0, STEPS, finish, 0)


def body(
    n_tm,
    features, rec_start, rec_end, w_value, w_gate, depth_kernel, norm_gain, norm_shift, w_down,
):
    frames, width = features.shape
    depth = w_value.shape[0]
    rows = frames // 2
    dma = pltpu.SemaphoreType.DMA
    vmem = pl.BlockSpec(memory_space=pltpu.VMEM)
    n_blocks = 2 * n_tm
    return pl.pallas_call(
        functools.partial(kernel, n_tm),
        out_shape=jax.ShapeDtypeStruct((frames, width), BF16),
        in_specs=[pl.BlockSpec(memory_space=pltpu.HBM)] * 9,
        out_specs=vmem,
        scratch_shapes=[
            pltpu.VMEM((depth, width), BF16),
            pltpu.VMEM((depth, width), BF16),
            pltpu.VMEM((frames // LANES, LANES), jnp.int32),
            pltpu.VMEM((frames // LANES, LANES), jnp.int32),
            pltpu.VMEM(depth_kernel.shape, BF16),
            pltpu.VMEM((width,), BF16),
            pltpu.VMEM((width,), BF16),
            pltpu.VMEM((4, rows, width), BF16),
            pltpu.VMEM((2, depth, width), BF16),
            pltpu.VMEM((2, 4 * width, width), BF16),
            pltpu.VMEM((width // GROUP, 4 * width), BF16),
            pltpu.VMEM((4, 16, LANES), F32),
            pltpu.VMEM((rows, LANES), F32),
            pltpu.VMEM((rows, LANES), F32),
            pltpu.VMEM((4, rows + 2 * PAD, LANES), F32),
            pltpu.VMEM((4, rows, LANES), F32),
            pltpu.VMEM((n_blocks, 8, LANES), F32),
            pltpu.VMEM((8, LANES), F32),
            pltpu.VMEM((2, 2, rows, width), BF16),
            pltpu.VMEM((rows, width), BF16),
            dma((12,)),
            dma((2,)), dma((2,)),
            dma((2, GROUP)), dma((2, GROUP)),
            dma, dma,
            dma((PARTS,)), dma((PARTS,)),
            dma((PARTS,)), dma((PARTS,)),
            dma((PARTS,)), dma((PARTS,)),
            dma((2, 2)), dma((2, 2)),
            dma, dma,
            dma((2,)), dma((2,)),
            dma((2, GROUP, 2)), dma((2, GROUP, 2)),
            dma, dma,
            dma((STEPS,)), dma((STEPS,)),
            dma((STEPS,)), dma((STEPS,)),
        ],
        compiler_params=pltpu.CompilerParams(
            collective_id=0, has_side_effects=True, vmem_limit_bytes=62 * 1024 * 1024
        ),
    )(
        features,
        rec_start.reshape(-1, LANES),
        rec_end.reshape(-1, LANES),
        w_value,
        w_gate,
        depth_kernel,
        norm_gain,
        norm_shift,
        w_down,
    )


def solution(mesh):
    in_specs = (
        P("tm", "chan"),
        P("tm"),
        P("tm"),
        P(None, "chan"),
        P(None, "chan"),
        P(None, "chan"),
        P("chan"),
        P("chan"),
        P("chan", None),
    )
    return jax.shard_map(
        functools.partial(body, mesh.shape["tm"]),
        mesh=mesh,
        in_specs=in_specs,
        out_specs=P("tm", "chan"),
        check_vma=False,
    )
```

```python
import functools

import jax
import jax.numpy as jnp
from jax import lax
from jax.experimental import pallas as pl
from jax.experimental.pallas import tpu as pltpu
from jax.sharding import PartitionSpec as P

F32, BF16 = jnp.float32, jnp.bfloat16
GROUP = 4
PARTS = 4
STEPS = 8
PAD = 8
BLOCK = 64
LANES = 128


def swish_gate(value, gate):
    return value * (0.5 * jnp.tanh(0.5 * gate) + 0.5)


def kernel(
    n_tm,
    feat, starts_in, ends_in, wv_in, wg_in, taps_in, gain_in, shift_in, wdown,
    out,
    wv, wg, starts, ends, taps, gain, shift,
    xg, wo, wd, wdx, par, back, fwd, glu, conv, stat, norm, sw, ob,
    loc, wy_s, wy_r, wf_s, wf_r, par_s, par_r, fc_s, fc_r, fy_s, fy_r, ff_s, ff_r,
    ha_s, ha_r, wx_s, wx_r, wb_s, wb_r, wd_s, wd_r, st_s, st_r, sw_s, sw_r, oy_s, oy_r,
):
    depth, width = wv.shape
    rows = feat.shape[0] // 2
    part, step_rows = rows // PARTS, rows // STEPS
    piece = depth // GROUP
    n_tap = taps.shape[0]
    reach = n_tap // 2
    n_blocks = 2 * n_tm
    total = n_blocks * rows

    t, chan = lax.axis_index("tm"), lax.axis_index("chan")
    y, core = chan // 2, chan % 2
    oy = 1 - y
    me = 2 * t + y
    across = (t, 2 * oy + core)
    beside = (t, 2 * y + 1 - core)
    group, g = t - t % GROUP, t % GROUP

    def at_block(b):
        return (b // 2, 2 * (b % 2) + core)

    def send(src, dst, s, r, to):
        return pltpu.make_async_remote_copy(
            src_ref=src, dst_ref=dst, send_sem=s, recv_sem=r,
            device_id=to, device_id_type=pl.DeviceIdType.MESH,
        )

    def landed(ref, sem):
        pltpu.make_async_copy(ref, ref, sem).wait()

    keep = pltpu.make_async_copy(
        feat.at[pl.ds(pl.multiple_of(y * rows, rows), rows)], xg.at[chan], loc.at[0]
    )
    loads = [
        pltpu.make_async_copy(src, dst, loc.at[3 + i])
        for i, (src, dst) in enumerate(
            (
                (starts_in, starts),
                (ends_in, ends),
                (taps_in, taps),
                (gain_in, gain),
                (shift_in, shift),
                (wv_in, wv),
                (wg_in, wg),
            )
        )
    ]
    for copy in loads:
        copy.start()
    keep.start()

    barrier = pltpu.get_barrier_semaphore()

    def greet(i, c):
        pl.semaphore_signal(
            barrier, inc=1, device_id=at_block((me + i) % n_blocks),
            device_id_type=pl.DeviceIdType.MESH,
        )
        return c

    lax.fori_loop(1, n_blocks, greet, 0)
    for i in range(GROUP):
        pl.semaphore_signal(
            barrier, inc=1, device_id=(group + (g + i) % GROUP, beside[1]),
            device_id_type=pl.DeviceIdType.MESH,
        )
    pl.semaphore_wait(barrier, n_blocks - 1 + GROUP)

    mine = pl.ds(pl.multiple_of(g * piece, piece), piece)
    cross = [
        send(w.at[mine], wo.at[k, mine], wy_s.at[k], wy_r.at[k], across)
        for k, w in enumerate((wv_in, wg_in))
    ]
    cross[0].start()

    def own_rows(i):
        return pl.ds(pl.multiple_of(y * rows + i * part, part), part)

    def other_rows(i):
        return pl.ds(pl.multiple_of(oy * rows + i * part, part), part)

    def part_rows(i):
        return pl.ds(pl.multiple_of(i * part, part), part)

    def order(i):
        return (3 * i) % PARTS

    def feat_beside(i):
        return send(
            feat.at[own_rows(i)], xg.at[chan, part_rows(i)], fc_s.at[i], fc_r.at[i], beside
        )

    def feat_across(i):
        return send(
            feat.at[other_rows(i)], xg.at[chan, part_rows(i)], fy_s.at[i], fy_r.at[i], across
        )

    def feat_forward(i):
        slot = 2 * oy + core
        return send(
            xg.at[slot, part_rows(i)], xg.at[slot, part_rows(i)], ff_s.at[i], ff_r.at[i], beside
        )

    for i in range(PARTS):
        feat_beside(order(i)).start()

    cross[0].wait_send()
    cross[1].start()
    for copy in loads[:5]:
        copy.wait()
    gain_row = gain[...].astype(F32).reshape(1, width)
    shift_row = shift[...].astype(F32).reshape(1, width)
    for q in range(2):
        lanes = slice(q * LANES, (q + 1) * LANES)
        par[2 * y + q] = jnp.zeros(par.shape[1:], F32)
        par[2 * y + q, 0:n_tap, :] = taps[:, lanes].astype(F32)
        par[2 * y + q, n_tap : n_tap + 1, :] = gain_row[:, lanes]
        par[2 * y + q, n_tap + 1 : n_tap + 2, :] = shift_row[:, lanes]
    my_par = par.at[pl.ds(2 * y, 2)]
    par_copy = send(my_par, my_par, par_s, par_r, across)
    par_copy.start()

    groups = rows // LANES
    base = t * 2 * rows + y * rows
    span = pl.ds(pl.multiple_of(y * groups, groups), groups)
    frame = (
        base
        + lax.broadcasted_iota(jnp.int32, (groups, LANES), 0) * LANES
        + lax.broadcasted_iota(jnp.int32, (groups, LANES), 1)
    )
    before = jnp.minimum(frame - starts[span, :], reach).astype(F32)
    after = jnp.minimum(ends[span, :] - 1 - frame, reach).astype(F32)
    for r in range(groups):
        tile = slice(r * LANES, (r + 1) * LANES)
        back[tile, :] = jnp.broadcast_to(before[r : r + 1, :], (LANES, LANES)).T
        fwd[tile, :] = jnp.broadcast_to(after[r : r + 1, :], (LANES, LANES)).T

    near = (g + 1 - 2 * (g % 2), (g + 2) % GROUP)

    def share(k, i):
        return send(
            wo.at[k, mine], wo.at[k, mine], wf_s.at[k, i], wf_r.at[k, i],
            (group + near[i], chan),
        )

    def relay(k, i):
        held = pl.ds(pl.multiple_of(near[i] * piece + i * (piece // 2), piece // 2), piece // 2)
        return send(
            wo.at[k, held], wo.at[k, held], wf_s.at[k, 2 + i], wf_r.at[k, 2 + i],
            (group + near[1 - i], chan),
        )

    for k in range(2):
        cross[k].wait_recv()
        for i in range(2):
            share(k, i).start()
        if k == 0:
            cross[1].wait_send()
            feat_across(order(0)).start()
    for i in range(1, PARTS):
        feat_across(order(i)).start()
    keep.wait()
    for copy in loads[5:]:
        copy.wait()
    for k in range(2):
        for i in range(2):
            share(k, i).wait_recv()
            relay(k, i).start()

    def gated(i, half, value_w, gate_w):
        x = jnp.concatenate([xg[j, part_rows(i), :] for j in range(4)], axis=1)
        value = jnp.dot(x, value_w, preferred_element_type=F32)
        gate = jnp.dot(x, gate_w, preferred_element_type=F32)
        both = swish_gate(value, gate).astype(BF16).astype(F32)
        to = pl.ds(pl.multiple_of(PAD + i * part, PAD), part)
        glu[2 * half, to, :] = both[:, :LANES]
        glu[2 * half + 1, to, :] = both[:, LANES:]

    def first_half(i):
        feat_across(i).wait_recv()
        feat_forward(i).start()
        feat_beside(i).wait_recv()
        feat_forward(i).wait_recv()
        gated(i, y, wv[...], wg[...])

    def second_half(i):
        gated(i, oy, wo[0], wo[1])

    def halos(half):
        pair = pl.ds(2 * half, 2)
        return (
            send(
                glu.at[pair, pl.ds(rows, PAD)], glu.at[pair, pl.ds(0, PAD)],
                ha_s.at[half, 0], ha_r.at[half, 0], at_block((me + 1) % n_blocks),
            ),
            send(
                glu.at[pair, pl.ds(PAD, PAD)], glu.at[pair, pl.ds(rows + PAD, PAD)],
                ha_s.at[half, 1], ha_r.at[half, 1], at_block((me + n_blocks - 1) % n_blocks),
            ),
        )

    down_piece = width // GROUP
    cut = pl.ds(pl.multiple_of(g * down_piece, down_piece), down_piece)
    down_cross = send(wdown.at[cut], wdx, wx_s, wx_r, across)

    def down_cols(h, c):
        return pl.ds(pl.multiple_of((2 * h + c) * width, width), width)

    own_held = pl.ds(pl.multiple_of(chan * width, width), width)

    def down_beside(h):
        return send(
            wdown.at[:, down_cols(h, 1 - core)], wd.at[h, own_held], wb_s.at[h], wb_r.at[h], beside
        )

    def down_keep(h):
        return pltpu.make_async_copy(
            wdown.at[:, down_cols(h, core)], wd.at[h, own_held], loc.at[1 + h]
        )

    def down_share(o, i, h):
        to_core = (core, 1 - core)[o]
        held = pl.ds(
            pl.multiple_of(across[1] * width + g * down_piece, down_piece), down_piece
        )
        src, dst = wdx.at[:, down_cols(h, to_core)], wd.at[h, held]
        if o == 0 and i == 0:
            return pltpu.make_async_copy(src, dst, loc.at[10 + h])
        to = (group + (g + i) % GROUP, 2 * y + to_core)
        return send(src, dst, wd_s.at[o, i, h], wd_r.at[o, i, h], to)

    shares = [
        (o, i, h) for i in (1, 2, 3, 0) for o in range(2) for h in range(2) if (o, i) != (0, 0)
    ]
    kept = [(0, 0, h) for h in range(2)]

    def convolve(q, b):
        at = pl.multiple_of(b * BLOCK, BLOCK)
        room_back, room_fwd = back[pl.ds(at, BLOCK), :], fwd[pl.ds(at, BLOCK), :]
        acc = jnp.zeros((BLOCK, LANES), F32)
        for k in range(n_tap):
            d = k - reach
            term = glu[q, pl.ds(at + (PAD + d), BLOCK), :] * par[q, k : k + 1, :]
            if d < 0:
                term = jnp.where(room_back >= float(-d), term, 0.0)
            elif d > 0:
                term = jnp.where(room_fwd >= float(d), term, 0.0)
            acc = acc + term
        conv[q, pl.ds(at, BLOCK), :] = acc

    last = order(PARTS - 1)
    n_inner = rows // BLOCK
    low, high = last * part // BLOCK - 1, (last + 1) * part // BLOCK + 1

    def inner(half):
        def run(b, c):
            for q in range(2):
                convolve(2 * half + q, b)
            return c

        return run

    first, final = order(0), order(1)
    first_half(first)
    first_half(final)
    for copy in halos(y):
        copy.start()
    for k in range(2):
        for i in range(2):
            relay(k, i).wait_recv()
    second_half(first)
    second_half(final)
    for copy in halos(oy):
        copy.start()
    for h in range(2):
        down_keep(h).start()
        down_beside(h).start()
    for n in range(2, PARTS - 1):
        first_half(order(n))
        if n == PARTS - 2:
            down_cross.start()
        second_half(order(n))
    par_copy.wait_recv()
    for half in (y, oy):
        for copy in halos(half):
            copy.wait_recv()
        lax.fori_loop(0, low, inner(half), 0)
        lax.fori_loop(high, n_inner, inner(half), 0)
    down_cross.wait_recv()
    for key in shares + kept:
        down_share(*key).start()
    first_half(last)
    second_half(last)
    for half in (y, oy):
        lax.fori_loop(low, high, inner(half), 0)

    for q in range(4):
        block = conv[q]
        total_q = jnp.sum(block, axis=0, keepdims=True)
        off = block - total_q * (1.0 / rows)
        stat[me, q : q + 1, :] = total_q
        stat[me, 4 + q : 5 + q, :] = jnp.sum(off * off, axis=0, keepdims=True)

    def tell(i, c):
        send(stat.at[me], stat.at[me], st_s, st_r, at_block((me + i) % n_blocks)).start()
        return c

    lax.fori_loop(1, n_blocks, tell, 0)
    landed(stat.at[pl.ds(0, n_blocks - 1)], st_r)
    sums, squares = stat[:, 0:4, :], stat[:, 4:8, :]
    mean = jnp.sum(sums, axis=0) * (1.0 / total)
    drift = sums * (1.0 / rows) - mean[None]
    var = jnp.sum(squares + float(rows) * (drift * drift), axis=0) * (1.0 / total)
    norm[0:4, :] = mean
    norm[4:8, :] = 1.0 / jnp.sqrt(var + 1e-05)

    def step_at(c):
        return pl.ds(pl.multiple_of(c * step_rows, step_rows), step_rows)

    def pass_on(c):
        mid = sw.at[core, :, step_at(c)]
        return send(mid, mid, sw_s.at[c], sw_r.at[c], beside)

    def activate(c):
        for q in range(4):
            scale = norm[4 + q : 5 + q, :] * par[q, n_tap : n_tap + 1, :]
            x = (conv[q, step_at(c), :] - norm[q : q + 1, :]) * scale
            x = x + par[q, n_tap + 1 : n_tap + 2, :]
            lanes = slice((q % 2) * LANES, (q % 2 + 1) * LANES)
            sw[core, q // 2, step_at(c), lanes] = swish_gate(x, x).astype(BF16)
        pass_on(c).start()

    def home_rows(c):
        return pl.ds(pl.multiple_of(y * rows + c * step_rows, step_rows), step_rows)

    def give(c):
        return send(ob.at[step_at(c)], out.at[home_rows(c)], oy_s.at[c], oy_r.at[c], across)

    def project(c):
        pass_on(c).wait_recv()
        x = jnp.concatenate([sw[j % 2, j // 2, step_at(c), :] for j in range(4)], axis=1)
        ob[step_at(c), :] = jnp.dot(x, wd[oy], preferred_element_type=F32).astype(BF16)
        give(c).start()
        out[home_rows(c), :] = jnp.dot(x, wd[y], preferred_element_type=F32).astype(BF16)

    activate(0)
    for h in range(2):
        down_keep(h).wait()
        down_beside(h).wait_recv()
    for key in shares:
        down_share(*key).wait_recv()
    for key in kept:
        down_share(*key).wait()

    def advance(c, carry):
        activate(c + 1)
        project(c)
        return carry

    lax.fori_loop(0, STEPS - 1, advance, 0)
    project(STEPS - 1)

    par_copy.wait_send()
    for half in (y, oy):
        for copy in halos(half):
            copy.wait_send()
    for k in range(2):
        for i in range(2):
            share(k, i).wait_send()
            relay(k, i).wait_send()
    down_cross.wait_send()
    for h in range(2):
        down_beside(h).wait_send()
    for key in shares:
        down_share(*key).wait_send()
    landed(stat.at[pl.ds(0, n_blocks - 1)], st_s)

    def drain(i, c):
        feat_beside(i).wait_send()
        feat_across(i).wait_send()
        feat_forward(i).wait_send()
        return c

    lax.fori_loop(0, PARTS, drain, 0)

    def finish(c, carry):
        pass_on(c).wait_send()
        give(c).wait()
        return carry

    lax.fori_loop(0, STEPS, finish, 0)


def body(
    n_tm,
    features, rec_start, rec_end, w_value, w_gate, depth_kernel, norm_gain, norm_shift, w_down,
):
    frames, width = features.shape
    depth = w_value.shape[0]
    rows = frames // 2
    dma = pltpu.SemaphoreType.DMA
    vmem = pl.BlockSpec(memory_space=pltpu.VMEM)
    n_blocks = 2 * n_tm
    return pl.pallas_call(
        functools.partial(kernel, n_tm),
        out_shape=jax.ShapeDtypeStruct((frames, width), BF16),
        in_specs=[pl.BlockSpec(memory_space=pltpu.HBM)] * 9,
        out_specs=vmem,
        scratch_shapes=[
            pltpu.VMEM((depth, width), BF16),
            pltpu.VMEM((depth, width), BF16),
            pltpu.VMEM((frames // LANES, LANES), jnp.int32),
            pltpu.VMEM((frames // LANES, LANES), jnp.int32),
            pltpu.VMEM(depth_kernel.shape, BF16),
            pltpu.VMEM((width,), BF16),
            pltpu.VMEM((width,), BF16),
            pltpu.VMEM((4, rows, width), BF16),
            pltpu.VMEM((2, depth, width), BF16),
            pltpu.VMEM((2, 4 * width, width), BF16),
            pltpu.VMEM((width // GROUP, 4 * width), BF16),
            pltpu.VMEM((4, 16, LANES), F32),
            pltpu.VMEM((rows, LANES), F32),
            pltpu.VMEM((rows, LANES), F32),
            pltpu.VMEM((4, rows + 2 * PAD, LANES), F32),
            pltpu.VMEM((4, rows, LANES), F32),
            pltpu.VMEM((n_blocks, 8, LANES), F32),
            pltpu.VMEM((8, LANES), F32),
            pltpu.VMEM((2, 2, rows, width), BF16),
            pltpu.VMEM((rows, width), BF16),
            dma((12,)),
            dma((2,)), dma((2,)),
            dma((2, GROUP)), dma((2, GROUP)),
            dma, dma,
            dma((PARTS,)), dma((PARTS,)),
            dma((PARTS,)), dma((PARTS,)),
            dma((PARTS,)), dma((PARTS,)),
            dma((2, 2)), dma((2, 2)),
            dma, dma,
            dma((2,)), dma((2,)),
            dma((2, GROUP, 2)), dma((2, GROUP, 2)),
            dma, dma,
            dma((STEPS,)), dma((STEPS,)),
            dma((STEPS,)), dma((STEPS,)),
        ],
        compiler_params=pltpu.CompilerParams(
            collective_id=0, has_side_effects=True, vmem_limit_bytes=62 * 1024 * 1024
        ),
    )(
        features,
        rec_start.reshape(-1, LANES),
        rec_end.reshape(-1, LANES),
        w_value,
        w_gate,
        depth_kernel,
        norm_gain,
        norm_shift,
        w_down,
    )


def solution(mesh):
    in_specs = (
        P("tm", "chan"),
        P("tm"),
        P("tm"),
        P(None, "chan"),
        P(None, "chan"),
        P(None, "chan"),
        P("chan"),
        P("chan"),
        P("chan", None),
    )
    return jax.shard_map(
        functools.partial(body, mesh.shape["tm"]),
        mesh=mesh,
        in_specs=in_specs,
        out_specs=P("tm", "chan"),
        check_vma=False,
    )
```

```python
import functools

import jax
import jax.numpy as jnp
from jax import lax
from jax.experimental import pallas as pl
from jax.experimental.pallas import tpu as pltpu
from jax.sharding import PartitionSpec as P

F32, BF16 = jnp.float32, jnp.bfloat16
GROUP = 4
PARTS = 8
STEPS = 8
PAD = 8
BLOCK = 64
LANES = 128


def swish_gate(value, gate):
    return value * (0.5 * jnp.tanh(0.5 * gate) + 0.5)


def kernel(
    n_tm,
    feat, starts_in, ends_in, wv_in, wg_in, taps_in, gain_in, shift_in, wdown,
    out,
    wv, wg, starts, ends, taps, gain, shift,
    xg, wo, wd, wdx, par, back, fwd, glu, conv, stat, norm, sw, ob,
    loc, wy_s, wy_r, wf_s, wf_r, par_s, par_r, fc_s, fc_r, fy_s, fy_r, ff_s, ff_r,
    ha_s, ha_r, wx_s, wx_r, wb_s, wb_r, wd_s, wd_r, st_s, st_r, sw_s, sw_r, oy_s, oy_r,
):
    depth, width = wv.shape
    rows = feat.shape[0] // 2
    part, step_rows = rows // PARTS, rows // STEPS
    piece = depth // GROUP
    n_tap = taps.shape[0]
    reach = n_tap // 2
    n_blocks = 2 * n_tm
    total = n_blocks * rows

    t, chan = lax.axis_index("tm"), lax.axis_index("chan")
    y, core = chan // 2, chan % 2
    oy = 1 - y
    me = 2 * t + y
    across = (t, 2 * oy + core)
    beside = (t, 2 * y + 1 - core)
    group, g = t - t % GROUP, t % GROUP

    def at_block(b):
        return (b // 2, 2 * (b % 2) + core)

    def send(src, dst, s, r, to):
        return pltpu.make_async_remote_copy(
            src_ref=src, dst_ref=dst, send_sem=s, recv_sem=r,
            device_id=to, device_id_type=pl.DeviceIdType.MESH,
        )

    def landed(ref, sem):
        pltpu.make_async_copy(ref, ref, sem).wait()

    keep = pltpu.make_async_copy(
        feat.at[pl.ds(pl.multiple_of(y * rows, rows), rows)], xg.at[chan], loc.at[0]
    )
    loads = [
        pltpu.make_async_copy(src, dst, loc.at[3 + i])
        for i, (src, dst) in enumerate(
            (
                (starts_in, starts),
                (ends_in, ends),
                (taps_in, taps),
                (gain_in, gain),
                (shift_in, shift),
                (wv_in, wv),
                (wg_in, wg),
            )
        )
    ]
    for copy in loads:
        copy.start()
    keep.start()

    barrier = pltpu.get_barrier_semaphore()

    def greet(i, c):
        pl.semaphore_signal(
            barrier, inc=1, device_id=at_block((me + i) % n_blocks),
            device_id_type=pl.DeviceIdType.MESH,
        )
        return c

    lax.fori_loop(1, n_blocks, greet, 0)
    for i in range(GROUP):
        pl.semaphore_signal(
            barrier, inc=1, device_id=(group + (g + i) % GROUP, beside[1]),
            device_id_type=pl.DeviceIdType.MESH,
        )
    pl.semaphore_wait(barrier, n_blocks - 1 + GROUP)

    mine = pl.ds(pl.multiple_of(g * piece, piece), piece)
    cross = [
        send(w.at[mine], wo.at[k, mine], wy_s.at[k], wy_r.at[k], across)
        for k, w in enumerate((wv_in, wg_in))
    ]
    cross[0].start()

    def own_rows(i):
        return pl.ds(pl.multiple_of(y * rows + i * part, part), part)

    def other_rows(i):
        return pl.ds(pl.multiple_of(oy * rows + i * part, part), part)

    def part_rows(i):
        return pl.ds(pl.multiple_of(i * part, part), part)

    def order(n):
        return (0, PARTS - 1)[n] if n < 2 else n - 1

    def feat_beside(i):
        return send(
            feat.at[own_rows(i)], xg.at[chan, part_rows(i)], fc_s.at[i], fc_r.at[i], beside
        )

    def feat_across(i):
        return send(
            feat.at[other_rows(i)], xg.at[chan, part_rows(i)], fy_s.at[i], fy_r.at[i], across
        )

    def feat_forward(i):
        slot = 2 * oy + core
        return send(
            xg.at[slot, part_rows(i)], xg.at[slot, part_rows(i)], ff_s.at[i], ff_r.at[i], beside
        )

    for i in range(PARTS):
        feat_beside(order(i)).start()

    cross[0].wait_send()
    cross[1].start()
    for copy in loads[:5]:
        copy.wait()
    gain_row = gain[...].astype(F32).reshape(1, width)
    shift_row = shift[...].astype(F32).reshape(1, width)
    for q in range(2):
        lanes = slice(q * LANES, (q + 1) * LANES)
        par[2 * y + q] = jnp.zeros(par.shape[1:], F32)
        par[2 * y + q, 0:n_tap, :] = taps[:, lanes].astype(F32)
        par[2 * y + q, n_tap : n_tap + 1, :] = gain_row[:, lanes]
        par[2 * y + q, n_tap + 1 : n_tap + 2, :] = shift_row[:, lanes]
    my_par = par.at[pl.ds(2 * y, 2)]
    par_copy = send(my_par, my_par, par_s, par_r, across)
    par_copy.start()

    groups = rows // LANES
    base = t * 2 * rows + y * rows
    span = pl.ds(pl.multiple_of(y * groups, groups), groups)
    frame = (
        base
        + lax.broadcasted_iota(jnp.int32, (groups, LANES), 0) * LANES
        + lax.broadcasted_iota(jnp.int32, (groups, LANES), 1)
    )
    before = jnp.minimum(frame - starts[span, :], reach).astype(F32)
    after = jnp.minimum(ends[span, :] - 1 - frame, reach).astype(F32)
    for r in range(groups):
        tile = slice(r * LANES, (r + 1) * LANES)
        back[tile, :] = jnp.broadcast_to(before[r : r + 1, :], (LANES, LANES)).T
        fwd[tile, :] = jnp.broadcast_to(after[r : r + 1, :], (LANES, LANES)).T

    near = (g + 1 - 2 * (g % 2), (g + 2) % GROUP)

    def share(k, i):
        return send(
            wo.at[k, mine], wo.at[k, mine], wf_s.at[k, i], wf_r.at[k, i],
            (group + near[i], chan),
        )

    def relay(k, i):
        held = pl.ds(pl.multiple_of(near[i] * piece + i * (piece // 2), piece // 2), piece // 2)
        return send(
            wo.at[k, held], wo.at[k, held], wf_s.at[k, 2 + i], wf_r.at[k, 2 + i],
            (group + near[1 - i], chan),
        )

    for k in range(2):
        cross[k].wait_recv()
        for i in range(2):
            share(k, i).start()
        if k == 0:
            cross[1].wait_send()
            feat_across(order(0)).start()
    for i in range(1, PARTS):
        feat_across(order(i)).start()
    keep.wait()
    for copy in loads[5:]:
        copy.wait()
    for k in range(2):
        for i in range(2):
            share(k, i).wait_recv()
            relay(k, i).start()

    def gated(i, half, value_w, gate_w):
        x = jnp.concatenate([xg[j, part_rows(i), :] for j in range(4)], axis=1)
        value = jnp.dot(x, value_w, preferred_element_type=F32)
        gate = jnp.dot(x, gate_w, preferred_element_type=F32)
        both = swish_gate(value, gate).astype(BF16).astype(F32)
        to = pl.ds(pl.multiple_of(PAD + i * part, PAD), part)
        glu[2 * half, to, :] = both[:, :LANES]
        glu[2 * half + 1, to, :] = both[:, LANES:]

    def first_half(i):
        feat_across(i).wait_recv()
        feat_forward(i).start()
        feat_beside(i).wait_recv()
        feat_forward(i).wait_recv()
        gated(i, y, wv[...], wg[...])

    def second_half(i):
        gated(i, oy, wo[0], wo[1])

    def halos(half):
        pair = pl.ds(2 * half, 2)
        return (
            send(
                glu.at[pair, pl.ds(rows, PAD)], glu.at[pair, pl.ds(0, PAD)],
                ha_s.at[half, 0], ha_r.at[half, 0], at_block((me + 1) % n_blocks),
            ),
            send(
                glu.at[pair, pl.ds(PAD, PAD)], glu.at[pair, pl.ds(rows + PAD, PAD)],
                ha_s.at[half, 1], ha_r.at[half, 1], at_block((me + n_blocks - 1) % n_blocks),
            ),
        )

    down_piece = width // GROUP
    cut = pl.ds(pl.multiple_of(g * down_piece, down_piece), down_piece)
    down_cross = send(wdown.at[cut], wdx, wx_s, wx_r, across)

    def down_cols(h, c):
        return pl.ds(pl.multiple_of((2 * h + c) * width, width), width)

    own_held = pl.ds(pl.multiple_of(chan * width, width), width)

    def down_beside(h):
        return send(
            wdown.at[:, down_cols(h, 1 - core)], wd.at[h, own_held], wb_s.at[h], wb_r.at[h], beside
        )

    def down_keep(h):
        return pltpu.make_async_copy(
            wdown.at[:, down_cols(h, core)], wd.at[h, own_held], loc.at[1 + h]
        )

    def down_share(o, i, h):
        to_core = (core, 1 - core)[o]
        held = pl.ds(
            pl.multiple_of(across[1] * width + g * down_piece, down_piece), down_piece
        )
        src, dst = wdx.at[:, down_cols(h, to_core)], wd.at[h, held]
        if o == 0 and i == 0:
            return pltpu.make_async_copy(src, dst, loc.at[10 + h])
        to = (group + (g + i) % GROUP, 2 * y + to_core)
        return send(src, dst, wd_s.at[o, i, h], wd_r.at[o, i, h], to)

    shares = [
        (o, i, h) for i in (1, 2, 3, 0) for o in range(2) for h in range(2) if (o, i) != (0, 0)
    ]
    kept = [(0, 0, h) for h in range(2)]

    def convolve(q, b):
        at = pl.multiple_of(b * BLOCK, BLOCK)
        room_back, room_fwd = back[pl.ds(at, BLOCK), :], fwd[pl.ds(at, BLOCK), :]
        acc = jnp.zeros((BLOCK, LANES), F32)
        for k in range(n_tap):
            d = k - reach
            term = glu[q, pl.ds(at + (PAD + d), BLOCK), :] * par[q, k : k + 1, :]
            if d < 0:
                term = jnp.where(room_back >= float(-d), term, 0.0)
            elif d > 0:
                term = jnp.where(room_fwd >= float(d), term, 0.0)
            acc = acc + term
        conv[q, pl.ds(at, BLOCK), :] = acc

    n_inner = rows // BLOCK

    def inner(half):
        def run(b, c):
            for q in range(2):
                convolve(2 * half + q, b)
            return c

        return run

    early = PARTS // 2
    for n in range(early):
        first_half(order(n))
        if n == 1:
            for copy in halos(y):
                copy.start()
    for k in range(2):
        for i in range(2):
            relay(k, i).wait_recv()
    second_half(order(0))
    second_half(order(1))
    for copy in halos(oy):
        copy.start()
    for h in range(2):
        down_keep(h).start()
        down_beside(h).start()
    for n in range(2, early):
        second_half(order(n))
    par_copy.wait_recv()
    for half in (y, oy):
        for copy in halos(half):
            copy.wait_recv()
    top = (PARTS - 1) * part // BLOCK + 1
    done = 0
    for n in range(early, PARTS):
        first_half(order(n))
        if n == PARTS - 2:
            down_cross.start()
        if n == PARTS - 1:
            down_cross.wait_recv()
            for key in shares + kept:
                down_share(*key).start()
        second_half(order(n))
        ready = top if n == PARTS - 1 else n * part // BLOCK - 1
        for half in (y, oy):
            lax.fori_loop(done, ready, inner(half), 0)
            if n == early:
                lax.fori_loop(top, n_inner, inner(half), 0)
        done = ready

    for q in range(4):
        block = conv[q]
        total_q = jnp.sum(block, axis=0, keepdims=True)
        off = block - total_q * (1.0 / rows)
        stat[me, q : q + 1, :] = total_q
        stat[me, 4 + q : 5 + q, :] = jnp.sum(off * off, axis=0, keepdims=True)

    def tell(i, c):
        send(stat.at[me], stat.at[me], st_s, st_r, at_block((me + i) % n_blocks)).start()
        return c

    lax.fori_loop(1, n_blocks, tell, 0)
    landed(stat.at[pl.ds(0, n_blocks - 1)], st_r)
    sums, squares = stat[:, 0:4, :], stat[:, 4:8, :]
    mean = jnp.sum(sums, axis=0) * (1.0 / total)
    drift = sums * (1.0 / rows) - mean[None]
    var = jnp.sum(squares + float(rows) * (drift * drift), axis=0) * (1.0 / total)
    norm[0:4, :] = mean
    norm[4:8, :] = 1.0 / jnp.sqrt(var + 1e-05)

    def step_at(c):
        return pl.ds(pl.multiple_of(c * step_rows, step_rows), step_rows)

    def pass_on(c):
        mid = sw.at[core, :, step_at(c)]
        return send(mid, mid, sw_s.at[c], sw_r.at[c], beside)

    def activate(c):
        for q in range(4):
            scale = norm[4 + q : 5 + q, :] * par[q, n_tap : n_tap + 1, :]
            x = (conv[q, step_at(c), :] - norm[q : q + 1, :]) * scale
            x = x + par[q, n_tap + 1 : n_tap + 2, :]
            lanes = slice((q % 2) * LANES, (q % 2 + 1) * LANES)
            sw[core, q // 2, step_at(c), lanes] = swish_gate(x, x).astype(BF16)
        pass_on(c).start()

    def home_rows(c):
        return pl.ds(pl.multiple_of(y * rows + c * step_rows, step_rows), step_rows)

    def give(c):
        return send(ob.at[step_at(c)], out.at[home_rows(c)], oy_s.at[c], oy_r.at[c], across)

    def project(c):
        pass_on(c).wait_recv()
        x = jnp.concatenate([sw[j % 2, j // 2, step_at(c), :] for j in range(4)], axis=1)
        ob[step_at(c), :] = jnp.dot(x, wd[oy], preferred_element_type=F32).astype(BF16)
        give(c).start()
        out[home_rows(c), :] = jnp.dot(x, wd[y], preferred_element_type=F32).astype(BF16)

    activate(0)
    for h in range(2):
        down_keep(h).wait()
        down_beside(h).wait_recv()
    for key in shares:
        down_share(*key).wait_recv()
    for key in kept:
        down_share(*key).wait()

    def advance(c, carry):
        activate(c + 1)
        project(c)
        return carry

    lax.fori_loop(0, STEPS - 1, advance, 0)
    project(STEPS - 1)

    par_copy.wait_send()
    for half in (y, oy):
        for copy in halos(half):
            copy.wait_send()
    for k in range(2):
        for i in range(2):
            share(k, i).wait_send()
            relay(k, i).wait_send()
    down_cross.wait_send()
    for h in range(2):
        down_beside(h).wait_send()
    for key in shares:
        down_share(*key).wait_send()
    landed(stat.at[pl.ds(0, n_blocks - 1)], st_s)

    def drain(i, c):
        feat_beside(i).wait_send()
        feat_across(i).wait_send()
        feat_forward(i).wait_send()
        return c

    lax.fori_loop(0, PARTS, drain, 0)

    def finish(c, carry):
        pass_on(c).wait_send()
        give(c).wait()
        return carry

    lax.fori_loop(0, STEPS, finish, 0)


def settle(src, dst, sem):
    rows = src.shape[0] // STEPS
    copies = [
        pltpu.make_async_copy(
            src.at[pl.ds(i * rows, rows)], dst.at[pl.ds(i * rows, rows)], sem.at[i]
        )
        for i in range(STEPS)
    ]
    for copy in copies:
        copy.start()
    for copy in copies:
        copy.wait()


def body(
    n_tm,
    features, rec_start, rec_end, w_value, w_gate, depth_kernel, norm_gain, norm_shift, w_down,
):
    frames, width = features.shape
    depth = w_value.shape[0]
    rows = frames // 2
    dma = pltpu.SemaphoreType.DMA
    vmem = pl.BlockSpec(memory_space=pltpu.VMEM)
    n_blocks = 2 * n_tm
    mixed = pl.pallas_call(
        functools.partial(kernel, n_tm),
        out_shape=jax.ShapeDtypeStruct((frames, width), BF16),
        in_specs=[pl.BlockSpec(memory_space=pltpu.HBM)] * 9,
        out_specs=vmem,
        scratch_shapes=[
            pltpu.VMEM((depth, width), BF16),
            pltpu.VMEM((depth, width), BF16),
            pltpu.VMEM((frames // LANES, LANES), jnp.int32),
            pltpu.VMEM((frames // LANES, LANES), jnp.int32),
            pltpu.VMEM(depth_kernel.shape, BF16),
            pltpu.VMEM((width,), BF16),
            pltpu.VMEM((width,), BF16),
            pltpu.VMEM((4, rows, width), BF16),
            pltpu.VMEM((2, depth, width), BF16),
            pltpu.VMEM((2, 4 * width, width), BF16),
            pltpu.VMEM((width // GROUP, 4 * width), BF16),
            pltpu.VMEM((4, 16, LANES), F32),
            pltpu.VMEM((rows, LANES), F32),
            pltpu.VMEM((rows, LANES), F32),
            pltpu.VMEM((4, rows + 2 * PAD, LANES), F32),
            pltpu.VMEM((4, rows, LANES), F32),
            pltpu.VMEM((n_blocks, 8, LANES), F32),
            pltpu.VMEM((8, LANES), F32),
            pltpu.VMEM((2, 2, rows, width), BF16),
            pltpu.VMEM((rows, width), BF16),
            dma((12,)),
            dma((2,)), dma((2,)),
            dma((2, GROUP)), dma((2, GROUP)),
            dma, dma,
            dma((PARTS,)), dma((PARTS,)),
            dma((PARTS,)), dma((PARTS,)),
            dma((PARTS,)), dma((PARTS,)),
            dma((2, 2)), dma((2, 2)),
            dma, dma,
            dma((2,)), dma((2,)),
            dma((2, GROUP, 2)), dma((2, GROUP, 2)),
            dma, dma,
            dma((STEPS,)), dma((STEPS,)),
            dma((STEPS,)), dma((STEPS,)),
        ],
        compiler_params=pltpu.CompilerParams(
            collective_id=0, has_side_effects=True, vmem_limit_bytes=62 * 1024 * 1024
        ),
    )(
        features,
        rec_start.reshape(-1, LANES),
        rec_end.reshape(-1, LANES),
        w_value,
        w_gate,
        depth_kernel,
        norm_gain,
        norm_shift,
        w_down,
    )
    hbm = pl.BlockSpec(memory_space=pltpu.HBM)
    return pl.pallas_call(
        settle,
        out_shape=jax.ShapeDtypeStruct((frames, width), BF16),
        in_specs=[hbm],
        out_specs=hbm,
        scratch_shapes=[dma((STEPS,))],
        compiler_params=pltpu.CompilerParams(vmem_limit_bytes=62 * 1024 * 1024),
    )(mixed)


def solution(mesh):
    in_specs = (
        P("tm", "chan"),
        P("tm"),
        P("tm"),
        P(None, "chan"),
        P(None, "chan"),
        P(None, "chan"),
        P("chan"),
        P("chan"),
        P("chan", None),
    )
    return jax.shard_map(
        functools.partial(body, mesh.shape["tm"]),
        mesh=mesh,
        in_specs=in_specs,
        out_specs=P("tm", "chan"),
        check_vma=False,
    )
```

```python
import functools

import jax
import jax.numpy as jnp
from jax import lax
from jax.experimental import pallas as pl
from jax.experimental.pallas import tpu as pltpu
from jax.sharding import PartitionSpec as P

F32, BF16 = jnp.float32, jnp.bfloat16
GROUP = 4
PARTS = 4
UNITS = 2
STEPS = 4
PAD = 8
BLOCK = 64
LANES = 128


def swish_gate(value, gate):
    return value * (0.5 * jnp.tanh(0.5 * gate) + 0.5)


def kernel(
    n_tm,
    feat, starts_in, ends_in, wv_in, wg_in, taps_in, gain_in, shift_in, wdown,
    out,
    w, starts, ends, taps, gain, shift,
    xg, wd, wdx, par, gap, back, fwd, glu, conv, stat, norm, sw, ob,
    loc, wy_s, wy_r, wf_s, wf_r, par_s, par_r, fc_s, fc_r, fy_s, fy_r, ff_s, ff_r,
    ha_s, ha_r, wx_s, wx_r, wb_s, wb_r, wd_s, wd_r, st_s, st_r, sw_s, sw_r, oy_s, oy_r,
):
    depth, width = wv_in.shape
    rows = feat.shape[0] // 2
    part, step_rows = rows // PARTS, rows // STEPS
    piece = depth // GROUP
    n_tap = taps.shape[0]
    reach = n_tap // 2
    n_blocks = 2 * n_tm
    total = n_blocks * rows

    t, chan = lax.axis_index("tm"), lax.axis_index("chan")
    y, core = chan // 2, chan % 2
    oy = 1 - y
    me = 2 * t + y
    across = (t, 2 * oy + core)
    beside = (t, 2 * y + 1 - core)
    group, g = t - t % GROUP, t % GROUP

    def at_block(b):
        return (b // 2, 2 * (b % 2) + core)

    def send(src, dst, s, r, to):
        return pltpu.make_async_remote_copy(
            src_ref=src, dst_ref=dst, send_sem=s, recv_sem=r,
            device_id=to, device_id_type=pl.DeviceIdType.MESH,
        )

    def landed(ref, sem):
        pltpu.make_async_copy(ref, ref, sem).wait()

    keep = pltpu.make_async_copy(
        feat.at[pl.ds(pl.multiple_of(y * rows, rows), rows)], xg.at[chan], loc.at[0]
    )
    loads = [
        pltpu.make_async_copy(src, dst, loc.at[3 + i])
        for i, (src, dst) in enumerate(
            (
                (starts_in, starts),
                (ends_in, ends),
                (taps_in, taps),
                (gain_in, gain),
                (shift_in, shift),
                (wv_in, w.at[y, 0]),
                (wg_in, w.at[y, 1]),
            )
        )
    ]
    for copy in loads:
        copy.start()
    keep.start()

    barrier = pltpu.get_barrier_semaphore()

    def greet(i, c):
        pl.semaphore_signal(
            barrier, inc=1, device_id=at_block((me + i) % n_blocks),
            device_id_type=pl.DeviceIdType.MESH,
        )
        return c

    lax.fori_loop(1, n_blocks, greet, 0)
    for i in range(GROUP):
        pl.semaphore_signal(
            barrier, inc=1, device_id=(group + (g + i) % GROUP, beside[1]),
            device_id_type=pl.DeviceIdType.MESH,
        )
    pl.semaphore_wait(barrier, n_blocks - 1 + GROUP)

    mine = pl.ds(pl.multiple_of(g * piece, piece), piece)
    cross = [
        send(mat.at[mine], w.at[y, k, mine], wy_s.at[k], wy_r.at[k], across)
        for k, mat in enumerate((wv_in, wg_in))
    ]
    cross[0].start()

    def own_rows(i):
        return pl.ds(pl.multiple_of(y * rows + i * part, part), part)

    def other_rows(i):
        return pl.ds(pl.multiple_of(oy * rows + i * part, part), part)

    def part_rows(i):
        return pl.ds(pl.multiple_of(i * part, part), part)

    def feat_beside(i):
        return send(
            feat.at[own_rows(i)], xg.at[chan, part_rows(i)], fc_s.at[i], fc_r.at[i], beside
        )

    def feat_across(i):
        return send(
            feat.at[other_rows(i)], xg.at[chan, part_rows(i)], fy_s.at[i], fy_r.at[i], across
        )

    def feat_forward(i):
        slot = 2 * oy + core
        return send(
            xg.at[slot, part_rows(i)], xg.at[slot, part_rows(i)], ff_s.at[i], ff_r.at[i], beside
        )

    for i in range(PARTS):
        feat_beside(i).start()

    cross[0].wait_send()
    cross[1].start()
    for copy in loads[:5]:
        copy.wait()
    gain_row = gain[...].astype(F32).reshape(1, width)
    shift_row = shift[...].astype(F32).reshape(1, width)
    for q in range(2):
        lanes = slice(q * LANES, (q + 1) * LANES)
        par[2 * y + q] = jnp.zeros(par.shape[1:], F32)
        par[2 * y + q, 0:n_tap, :] = taps[:, lanes].astype(F32)
        par[2 * y + q, n_tap : n_tap + 1, :] = gain_row[:, lanes]
        par[2 * y + q, n_tap + 1 : n_tap + 2, :] = shift_row[:, lanes]
    my_par = par.at[pl.ds(2 * y, 2)]
    par_copy = send(my_par, my_par, par_s, par_r, across)
    par_copy.start()

    groups = rows // LANES
    base = t * 2 * rows + y * rows
    span = pl.ds(pl.multiple_of(y * groups, groups), groups)
    frame = (
        base
        + lax.broadcasted_iota(jnp.int32, (groups, LANES), 0) * LANES
        + lax.broadcasted_iota(jnp.int32, (groups, LANES), 1)
    )
    before = jnp.minimum(frame - starts[span, :], reach).astype(F32)
    after = jnp.minimum(ends[span, :] - 1 - frame, reach).astype(F32)
    gap[0], gap[1] = before, after

    def spread(r, c):
        tile = pl.ds(pl.multiple_of(r * LANES, LANES), LANES)
        back[tile, :] = jnp.broadcast_to(gap[0, pl.ds(r, 1), :], (LANES, LANES)).T
        fwd[tile, :] = jnp.broadcast_to(gap[1, pl.ds(r, 1), :], (LANES, LANES)).T
        return c

    lax.fori_loop(0, groups, spread, 0)

    near = (g + 1 - 2 * (g % 2), (g + 2) % GROUP)

    def share(k, i):
        return send(
            w.at[oy, k, mine], w.at[oy, k, mine], wf_s.at[k, i], wf_r.at[k, i],
            (group + near[i], chan),
        )

    def relay(k, i):
        held = pl.ds(pl.multiple_of(near[i] * piece + i * (piece // 2), piece // 2), piece // 2)
        return send(
            w.at[oy, k, held], w.at[oy, k, held], wf_s.at[k, 2 + i], wf_r.at[k, 2 + i],
            (group + near[1 - i], chan),
        )

    for k in range(2):
        cross[k].wait_recv()
        for i in range(2):
            share(k, i).start()
        if k == 0:
            cross[1].wait_send()
            feat_across(0).start()
    for i in range(1, PARTS):
        feat_across(i).start()
    keep.wait()
    for copy in loads[5:]:
        copy.wait()
    for k in range(2):
        for i in range(2):
            share(k, i).wait_recv()
            relay(k, i).start()

    unit = rows // UNITS
    per_unit = PARTS // UNITS

    def gated(i, half):
        at = pl.ds(pl.multiple_of(i * unit, unit), unit)
        x = jnp.concatenate([xg[j, at, :] for j in range(4)], axis=1)
        value = jnp.dot(x, w[half, 0], preferred_element_type=F32)
        gate = jnp.dot(x, w[half, 1], preferred_element_type=F32)
        both = swish_gate(value, gate).astype(BF16).astype(F32)
        to = pl.ds(pl.multiple_of(PAD + i * unit, PAD), unit)
        glu[2 * half, to, :] = both[:, :LANES]
        glu[2 * half + 1, to, :] = both[:, LANES:]

    def arrive(i):
        feat_across(i).wait_recv()
        feat_forward(i).start()
        feat_beside(i).wait_recv()

    def halos(half):
        pair = pl.ds(2 * half, 2)
        return (
            send(
                glu.at[pair, pl.ds(rows, PAD)], glu.at[pair, pl.ds(0, PAD)],
                ha_s.at[half, 0], ha_r.at[half, 0], at_block((me + 1) % n_blocks),
            ),
            send(
                glu.at[pair, pl.ds(PAD, PAD)], glu.at[pair, pl.ds(rows + PAD, PAD)],
                ha_s.at[half, 1], ha_r.at[half, 1], at_block((me + n_blocks - 1) % n_blocks),
            ),
        )

    down_piece = width // GROUP
    cut = pl.ds(pl.multiple_of(g * down_piece, down_piece), down_piece)
    down_cross = send(wdown.at[cut], wdx, wx_s, wx_r, across)

    def down_cols(h, c):
        return pl.ds(pl.multiple_of((2 * h + c) * width, width), width)

    own_held = pl.ds(pl.multiple_of(chan * width, width), width)

    def down_beside(h):
        return send(
            wdown.at[:, down_cols(h, 1 - core)], wd.at[h, own_held], wb_s.at[h], wb_r.at[h], beside
        )

    def down_keep(h):
        return pltpu.make_async_copy(
            wdown.at[:, down_cols(h, core)], wd.at[h, own_held], loc.at[1 + h]
        )

    def down_share(o, i, h):
        to_core = (core, 1 - core)[o]
        held = pl.ds(
            pl.multiple_of(across[1] * width + g * down_piece, down_piece), down_piece
        )
        src, dst = wdx.at[:, down_cols(h, to_core)], wd.at[h, held]
        if o == 0 and i == 0:
            return pltpu.make_async_copy(src, dst, loc.at[10 + h])
        to = (group + (g + i) % GROUP, 2 * y + to_core)
        return send(src, dst, wd_s.at[o, i, h], wd_r.at[o, i, h], to)

    shares = [
        (o, i, h) for i in (1, 2, 3, 0) for o in range(2) for h in range(2) if (o, i) != (0, 0)
    ]
    kept = [(0, 0, h) for h in range(2)]

    def convolve(q, b):
        at = pl.multiple_of(b * BLOCK, BLOCK)
        room_back, room_fwd = back[pl.ds(at, BLOCK), :], fwd[pl.ds(at, BLOCK), :]
        acc = jnp.zeros((BLOCK, LANES), F32)
        for k in range(n_tap):
            d = k - reach
            term = glu[q, pl.ds(at + (PAD + d), BLOCK), :] * par[q, k : k + 1, :]
            if d < 0:
                term = jnp.where(room_back >= float(-d), term, 0.0)
            elif d > 0:
                term = jnp.where(room_fwd >= float(d), term, 0.0)
            acc = acc + term
        conv[q, pl.ds(at, BLOCK), :] = acc

    n_inner = rows // BLOCK
    per_block = unit // BLOCK

    def inner(b, c):
        def one(q, c):
            convolve(q, b)
            return c

        return lax.fori_loop(0, 4, one, c)

    def settle(i, c):
        lax.fori_loop(i * per_unit, (i + 1) * per_unit, lambda n, c: arrive(n) or c, 0)

        @pl.when(i == UNITS - 1)
        def _():
            down_cross.start()

        lax.fori_loop(
            i * per_unit, (i + 1) * per_unit, lambda n, c: feat_forward(n).wait_recv() or c, 0
        )

        def product(j, c):
            @pl.when((i == 0) & (j == 1))
            def _():
                for k in range(2):
                    for n in range(2):
                        relay(k, n).wait_recv()

            gated(i, (y + j) % 2)
            return c

        lax.fori_loop(0, 2, product, 0)

        @pl.when(i == 0)
        def _():
            par_copy.wait_recv()
            for h in range(2):
                down_keep(h).start()
                down_beside(h).start()

        @pl.when(i == UNITS - 1)
        def _():
            for half in (y, oy):
                for copy in halos(half):
                    copy.start()

        low = jnp.where(i == 0, 1, i * per_block - 1)
        lax.fori_loop(low, (i + 1) * per_block - 1, inner, 0)
        return c

    lax.fori_loop(0, UNITS, settle, 0)
    down_cross.wait_recv()
    for key in shares + kept:
        down_share(*key).start()
    for half in (y, oy):
        for copy in halos(half):
            copy.wait_recv()
    lax.fori_loop(0, 2, lambda n, c: inner(n * (n_inner - 1), c), 0)

    def gather(q, c):
        block = conv[q]
        total_q = jnp.sum(block, axis=0, keepdims=True)
        off = block - total_q * (1.0 / rows)
        stat[me, pl.ds(q, 1), :] = total_q
        stat[me, pl.ds(4 + q, 1), :] = jnp.sum(off * off, axis=0, keepdims=True)
        return c

    lax.fori_loop(0, 4, gather, 0)

    def tell(i, c):
        send(stat.at[me], stat.at[me], st_s, st_r, at_block((me + i) % n_blocks)).start()
        return c

    lax.fori_loop(1, n_blocks, tell, 0)
    landed(stat.at[pl.ds(0, n_blocks - 1)], st_r)
    sums, squares = stat[:, 0:4, :], stat[:, 4:8, :]
    mean = jnp.sum(sums, axis=0) * (1.0 / total)
    drift = sums * (1.0 / rows) - mean[None]
    var = jnp.sum(squares + float(rows) * (drift * drift), axis=0) * (1.0 / total)
    norm[0:4, :] = mean
    norm[4:8, :] = 1.0 / jnp.sqrt(var + 1e-05)

    def step_at(c):
        return pl.ds(pl.multiple_of(c * step_rows, step_rows), step_rows)

    def pass_on(c):
        mid = sw.at[core, :, step_at(c)]
        return send(mid, mid, sw_s.at[c], sw_r.at[c], beside)

    def activate(c):
        for q in range(4):
            scale = norm[4 + q : 5 + q, :] * par[q, n_tap : n_tap + 1, :]
            x = (conv[q, step_at(c), :] - norm[q : q + 1, :]) * scale
            x = x + par[q, n_tap + 1 : n_tap + 2, :]
            lanes = slice((q % 2) * LANES, (q % 2 + 1) * LANES)
            sw[core, q // 2, step_at(c), lanes] = swish_gate(x, x).astype(BF16)
        pass_on(c).start()

    def home_rows(c):
        return pl.ds(pl.multiple_of(y * rows + c * step_rows, step_rows), step_rows)

    def give(c):
        return send(ob.at[step_at(c)], out.at[home_rows(c)], oy_s.at[c], oy_r.at[c], across)

    def project(c):
        pass_on(c).wait_recv()
        x = jnp.concatenate([sw[j % 2, j // 2, step_at(c), :] for j in range(4)], axis=1)
        ob[step_at(c), :] = jnp.dot(x, wd[oy], preferred_element_type=F32).astype(BF16)
        give(c).start()
        out[home_rows(c), :] = jnp.dot(x, wd[y], preferred_element_type=F32).astype(BF16)

    def ready():
        for h in range(2):
            down_keep(h).wait()
            down_beside(h).wait_recv()
        for key in shares:
            down_share(*key).wait_recv()
        for key in kept:
            down_share(*key).wait()

    def advance(c, carry):
        pl.when(c < STEPS)(lambda: activate(c))
        pl.when(c == 1)(ready)
        pl.when(c > 0)(lambda: project(c - 1))
        return carry

    lax.fori_loop(0, STEPS + 1, advance, 0)

    par_copy.wait_send()
    for half in (y, oy):
        for copy in halos(half):
            copy.wait_send()
    for k in range(2):
        for i in range(2):
            share(k, i).wait_send()
            relay(k, i).wait_send()
    down_cross.wait_send()
    for h in range(2):
        down_beside(h).wait_send()
    for key in shares:
        down_share(*key).wait_send()
    landed(stat.at[pl.ds(0, n_blocks - 1)], st_s)

    def drain(i, c):
        feat_beside(i).wait_send()
        feat_across(i).wait_send()
        feat_forward(i).wait_send()
        return c

    lax.fori_loop(0, PARTS, drain, 0)

    def finish(c, carry):
        pass_on(c).wait_send()
        give(c).wait()
        return carry

    lax.fori_loop(0, STEPS, finish, 0)


def body(
    n_tm,
    features, rec_start, rec_end, w_value, w_gate, depth_kernel, norm_gain, norm_shift, w_down,
):
    frames, width = features.shape
    depth = w_value.shape[0]
    rows = frames // 2
    dma = pltpu.SemaphoreType.DMA
    vmem = pl.BlockSpec(memory_space=pltpu.VMEM)
    n_blocks = 2 * n_tm
    return pl.pallas_call(
        functools.partial(kernel, n_tm),
        out_shape=jax.ShapeDtypeStruct((frames, width), BF16),
        in_specs=[pl.BlockSpec(memory_space=pltpu.HBM)] * 9,
        out_specs=vmem,
        scratch_shapes=[
            pltpu.VMEM((2, 2, depth, width), BF16),
            pltpu.VMEM((frames // LANES, LANES), jnp.int32),
            pltpu.VMEM((frames // LANES, LANES), jnp.int32),
            pltpu.VMEM(depth_kernel.shape, BF16),
            pltpu.VMEM((width,), BF16),
            pltpu.VMEM((width,), BF16),
            pltpu.VMEM((4, rows, width), BF16),
            pltpu.VMEM((2, 4 * width, width), BF16),
            pltpu.VMEM((width // GROUP, 4 * width), BF16),
            pltpu.VMEM((4, 16, LANES), F32),
            pltpu.VMEM((2, rows // LANES, LANES), F32),
            pltpu.VMEM((rows, LANES), F32),
            pltpu.VMEM((rows, LANES), F32),
            pltpu.VMEM((4, rows + 2 * PAD, LANES), F32),
            pltpu.VMEM((4, rows, LANES), F32),
            pltpu.VMEM((n_blocks, 8, LANES), F32),
            pltpu.VMEM((8, LANES), F32),
            pltpu.VMEM((2, 2, rows, width), BF16),
            pltpu.VMEM((rows, width), BF16),
            dma((12,)),
            dma((2,)), dma((2,)),
            dma((2, GROUP)), dma((2, GROUP)),
            dma, dma,
            dma((PARTS,)), dma((PARTS,)),
            dma((PARTS,)), dma((PARTS,)),
            dma((PARTS,)), dma((PARTS,)),
            dma((2, 2)), dma((2, 2)),
            dma, dma,
            dma((2,)), dma((2,)),
            dma((2, GROUP, 2)), dma((2, GROUP, 2)),
            dma, dma,
            dma((STEPS,)), dma((STEPS,)),
            dma((STEPS,)), dma((STEPS,)),
        ],
        compiler_params=pltpu.CompilerParams(
            collective_id=0, has_side_effects=True, vmem_limit_bytes=62 * 1024 * 1024
        ),
    )(
        features,
        rec_start.reshape(-1, LANES),
        rec_end.reshape(-1, LANES),
        w_value,
        w_gate,
        depth_kernel,
        norm_gain,
        norm_shift,
        w_down,
    )


def solution(mesh):
    in_specs = (
        P("tm", "chan"),
        P("tm"),
        P("tm"),
        P(None, "chan"),
        P(None, "chan"),
        P(None, "chan"),
        P("chan"),
        P("chan"),
        P("chan", None),
    )
    return jax.shard_map(
        functools.partial(body, mesh.shape["tm"]),
        mesh=mesh,
        in_specs=in_specs,
        out_specs=P("tm", "chan"),
        check_vma=False,
    )
```

```python
import functools

import jax
import jax.numpy as jnp
from jax import lax
from jax.experimental import pallas as pl
from jax.experimental.pallas import tpu as pltpu
from jax.sharding import PartitionSpec as P

F32, BF16 = jnp.float32, jnp.bfloat16
GROUP = 4
PARTS = 4
UNITS = 4
STEPS = 4
PAD = 8
BLOCK = 32
LANES = 128


def swish_gate(value, gate):
    return value * (0.5 * jnp.tanh(0.5 * gate) + 0.5)


def kernel(
    n_tm,
    feat, starts_in, ends_in, wv_in, wg_in, taps_in, gain_in, shift_in, wdown,
    out,
    w, starts, ends, taps, gain, shift,
    xg, wd, wdx, par, gap, back, fwd, glu, conv, stat, norm, sw, ob,
    loc, wy_s, wy_r, wf_s, wf_r, par_s, par_r, fc_s, fc_r, fy_s, fy_r, ff_s, ff_r,
    ha_s, ha_r, wx_s, wx_r, wb_s, wb_r, wd_s, wd_r, st_s, st_r, sw_s, sw_r, oy_s, oy_r,
):
    depth, width = wv_in.shape
    rows = feat.shape[0] // 2
    part, step_rows = rows // PARTS, rows // STEPS
    piece = depth // GROUP
    n_tap = taps.shape[0]
    reach = n_tap // 2
    n_blocks = 2 * n_tm
    total = n_blocks * rows

    t, chan = lax.axis_index("tm"), lax.axis_index("chan")
    y, core = chan // 2, chan % 2
    oy = 1 - y
    me = 2 * t + y
    across = (t, 2 * oy + core)
    beside = (t, 2 * y + 1 - core)
    group, g = t - t % GROUP, t % GROUP

    def at_block(b):
        return (b // 2, 2 * (b % 2) + core)

    def send(src, dst, s, r, to):
        return pltpu.make_async_remote_copy(
            src_ref=src, dst_ref=dst, send_sem=s, recv_sem=r,
            device_id=to, device_id_type=pl.DeviceIdType.MESH,
        )

    def landed(ref, sem):
        pltpu.make_async_copy(ref, ref, sem).wait()

    keep = pltpu.make_async_copy(
        feat.at[pl.ds(pl.multiple_of(y * rows, rows), rows)], xg.at[chan], loc.at[0]
    )
    loads = [
        pltpu.make_async_copy(src, dst, loc.at[3 + i])
        for i, (src, dst) in enumerate(
            (
                (starts_in, starts),
                (ends_in, ends),
                (taps_in, taps),
                (gain_in, gain),
                (shift_in, shift),
                (wv_in, w.at[y, 0]),
                (wg_in, w.at[y, 1]),
            )
        )
    ]
    for copy in loads:
        copy.start()
    keep.start()

    barrier = pltpu.get_barrier_semaphore()

    def greet(i, c):
        pl.semaphore_signal(
            barrier, inc=1, device_id=at_block((me + i) % n_blocks),
            device_id_type=pl.DeviceIdType.MESH,
        )
        return c

    lax.fori_loop(1, n_blocks, greet, 0)
    for i in range(GROUP):
        pl.semaphore_signal(
            barrier, inc=1, device_id=(group + (g + i) % GROUP, beside[1]),
            device_id_type=pl.DeviceIdType.MESH,
        )
    pl.semaphore_wait(barrier, n_blocks - 1 + GROUP)

    mine = pl.ds(pl.multiple_of(g * piece, piece), piece)
    cross = [
        send(mat.at[mine], w.at[y, k, mine], wy_s.at[k], wy_r.at[k], across)
        for k, mat in enumerate((wv_in, wg_in))
    ]
    cross[0].start()

    def own_rows(i):
        return pl.ds(pl.multiple_of(y * rows + i * part, part), part)

    def other_rows(i):
        return pl.ds(pl.multiple_of(oy * rows + i * part, part), part)

    def part_rows(i):
        return pl.ds(pl.multiple_of(i * part, part), part)

    def feat_beside(i):
        return send(
            feat.at[own_rows(i)], xg.at[chan, part_rows(i)], fc_s.at[i], fc_r.at[i], beside
        )

    def feat_across(i):
        return send(
            feat.at[other_rows(i)], xg.at[chan, part_rows(i)], fy_s.at[i], fy_r.at[i], across
        )

    def feat_forward(i):
        slot = 2 * oy + core
        return send(
            xg.at[slot, part_rows(i)], xg.at[slot, part_rows(i)], ff_s.at[i], ff_r.at[i], beside
        )

    for i in range(PARTS):
        feat_beside(i).start()

    cross[0].wait_send()
    cross[1].start()
    for copy in loads[:5]:
        copy.wait()
    gain_row = gain[...].astype(F32).reshape(1, width)
    shift_row = shift[...].astype(F32).reshape(1, width)
    for q in range(2):
        lanes = slice(q * LANES, (q + 1) * LANES)
        par[2 * y + q] = jnp.zeros(par.shape[1:], F32)
        par[2 * y + q, 0:n_tap, :] = taps[:, lanes].astype(F32)
        par[2 * y + q, n_tap : n_tap + 1, :] = gain_row[:, lanes]
        par[2 * y + q, n_tap + 1 : n_tap + 2, :] = shift_row[:, lanes]
    my_par = par.at[pl.ds(2 * y, 2)]
    par_copy = send(my_par, my_par, par_s, par_r, across)
    par_copy.start()

    groups = rows // LANES
    base = t * 2 * rows + y * rows
    span = pl.ds(pl.multiple_of(y * groups, groups), groups)
    frame = (
        base
        + lax.broadcasted_iota(jnp.int32, (groups, LANES), 0) * LANES
        + lax.broadcasted_iota(jnp.int32, (groups, LANES), 1)
    )
    before = jnp.minimum(frame - starts[span, :], reach).astype(F32)
    after = jnp.minimum(ends[span, :] - 1 - frame, reach).astype(F32)
    gap[0], gap[1] = before, after

    def spread(r, c):
        tile = pl.ds(pl.multiple_of(r * LANES, LANES), LANES)
        back[tile, :] = jnp.broadcast_to(gap[0, pl.ds(r, 1), :], (LANES, LANES)).T
        fwd[tile, :] = jnp.broadcast_to(gap[1, pl.ds(r, 1), :], (LANES, LANES)).T
        return c

    lax.fori_loop(0, groups, spread, 0)

    near = (g + 1 - 2 * (g % 2), (g + 2) % GROUP)

    def share(k, i):
        return send(
            w.at[oy, k, mine], w.at[oy, k, mine], wf_s.at[k, i], wf_r.at[k, i],
            (group + near[i], chan),
        )

    def relay(k, i):
        held = pl.ds(pl.multiple_of(near[i] * piece + i * (piece // 2), piece // 2), piece // 2)
        return send(
            w.at[oy, k, held], w.at[oy, k, held], wf_s.at[k, 2 + i], wf_r.at[k, 2 + i],
            (group + near[1 - i], chan),
        )

    for k in range(2):
        cross[k].wait_recv()
        for i in range(2):
            share(k, i).start()
        if k == 0:
            cross[1].wait_send()
            feat_across(0).start()
    for i in range(1, PARTS):
        feat_across(i).start()
    keep.wait()
    for copy in loads[5:]:
        copy.wait()
    for k in range(2):
        for i in range(2):
            share(k, i).wait_recv()
            relay(k, i).start()

    unit = rows // UNITS
    per_unit = PARTS // UNITS

    def gated(i, half):
        at = pl.ds(pl.multiple_of(i * unit, unit), unit)
        x = jnp.concatenate([xg[j, at, :] for j in range(4)], axis=1)
        value = jnp.dot(x, w[half, 0], preferred_element_type=F32)
        gate = jnp.dot(x, w[half, 1], preferred_element_type=F32)
        both = swish_gate(value, gate).astype(BF16).astype(F32)
        to = pl.ds(pl.multiple_of(PAD + i * unit, PAD), unit)
        glu[2 * half, to, :] = both[:, :LANES]
        glu[2 * half + 1, to, :] = both[:, LANES:]

    def arrive(i):
        feat_across(i).wait_recv()
        feat_forward(i).start()
        feat_beside(i).wait_recv()

    def halos(half):
        pair = pl.ds(2 * half, 2)
        return (
            send(
                glu.at[pair, pl.ds(rows, PAD)], glu.at[pair, pl.ds(0, PAD)],
                ha_s.at[half, 0], ha_r.at[half, 0], at_block((me + 1) % n_blocks),
            ),
            send(
                glu.at[pair, pl.ds(PAD, PAD)], glu.at[pair, pl.ds(rows + PAD, PAD)],
                ha_s.at[half, 1], ha_r.at[half, 1], at_block((me + n_blocks - 1) % n_blocks),
            ),
        )

    down_piece = width // GROUP
    cut = pl.ds(pl.multiple_of(g * down_piece, down_piece), down_piece)
    down_cross = send(wdown.at[cut], wdx, wx_s, wx_r, across)

    def down_cols(h, c):
        return pl.ds(pl.multiple_of((2 * h + c) * width, width), width)

    own_held = pl.ds(pl.multiple_of(chan * width, width), width)

    def down_beside(h):
        return send(
            wdown.at[:, down_cols(h, 1 - core)], wd.at[h, own_held], wb_s.at[h], wb_r.at[h], beside
        )

    def down_keep(h):
        return pltpu.make_async_copy(
            wdown.at[:, down_cols(h, core)], wd.at[h, own_held], loc.at[1 + h]
        )

    def down_share(o, i, h):
        to_core = (core, 1 - core)[o]
        held = pl.ds(
            pl.multiple_of(across[1] * width + g * down_piece, down_piece), down_piece
        )
        src, dst = wdx.at[:, down_cols(h, to_core)], wd.at[h, held]
        if o == 0 and i == 0:
            return pltpu.make_async_copy(src, dst, loc.at[10 + h])
        to = (group + (g + i) % GROUP, 2 * y + to_core)
        return send(src, dst, wd_s.at[o, i, h], wd_r.at[o, i, h], to)

    shares = [
        (o, i, h) for i in (1, 2, 3, 0) for o in range(2) for h in range(2) if (o, i) != (0, 0)
    ]
    kept = [(0, 0, h) for h in range(2)]

    def inner(b, c):
        at = pl.multiple_of(b * BLOCK, BLOCK)
        room_back, room_fwd = back[pl.ds(at, BLOCK), :], fwd[pl.ds(at, BLOCK), :]
        accs = [jnp.zeros((BLOCK, LANES), F32)] * 4
        for k in range(n_tap):
            d = k - reach
            usable = room_back >= float(-d) if d < 0 else room_fwd >= float(d)
            for q in range(4):
                term = glu[q, pl.ds(at + (PAD + d), BLOCK), :] * par[q, k : k + 1, :]
                accs[q] = accs[q] + (term if d == 0 else jnp.where(usable, term, 0.0))
        for q in range(4):
            conv[q, pl.ds(at, BLOCK), :] = accs[q]
        return c

    n_inner = rows // BLOCK
    per_block = unit // BLOCK

    def settle(i, c):
        @pl.when(i < UNITS)
        def _():
            lax.fori_loop(i * per_unit, (i + 1) * per_unit, lambda n, c: arrive(n) or c, 0)

        @pl.when(i == UNITS - 1)
        def _():
            down_cross.start()

        @pl.when(i == 1)
        def _():
            for k in range(2):
                for n in range(2):
                    relay(k, n).wait_recv()
            par_copy.wait_recv()
            for h in range(2):
                down_keep(h).start()
                down_beside(h).start()

        @pl.when(i > 0)
        def _():
            u = i - 1
            gated(u, oy)

            @pl.when(u == UNITS - 1)
            def _():
                for half in (y, oy):
                    for copy in halos(half):
                        copy.start()

            low = jnp.where(u == 0, 1, u * per_block - 1)
            lax.fori_loop(low, (u + 1) * per_block - 1, inner, 0)

        @pl.when(i < UNITS)
        def _():
            lax.fori_loop(
                i * per_unit, (i + 1) * per_unit, lambda n, c: feat_forward(n).wait_recv() or c, 0
            )
            gated(i, y)

        return c

    lax.fori_loop(0, UNITS + 1, settle, 0)
    down_cross.wait_recv()
    for key in shares + kept:
        down_share(*key).start()
    for half in (y, oy):
        for copy in halos(half):
            copy.wait_recv()
    lax.fori_loop(0, 2, lambda n, c: inner(n * (n_inner - 1), c), 0)

    def gather(q, c):
        block = conv[q]
        total_q = jnp.sum(block, axis=0, keepdims=True)
        off = block - total_q * (1.0 / rows)
        stat[me, pl.ds(q, 1), :] = total_q
        stat[me, pl.ds(4 + q, 1), :] = jnp.sum(off * off, axis=0, keepdims=True)
        return c

    lax.fori_loop(0, 4, gather, 0)

    def tell(i, c):
        send(stat.at[me], stat.at[me], st_s, st_r, at_block((me + i) % n_blocks)).start()
        return c

    lax.fori_loop(1, n_blocks, tell, 0)
    landed(stat.at[pl.ds(0, n_blocks - 1)], st_r)
    sums, squares = stat[:, 0:4, :], stat[:, 4:8, :]
    mean = jnp.sum(sums, axis=0) * (1.0 / total)
    drift = sums * (1.0 / rows) - mean[None]
    var = jnp.sum(squares + float(rows) * (drift * drift), axis=0) * (1.0 / total)
    norm[0:4, :] = mean
    norm[4:8, :] = 1.0 / jnp.sqrt(var + 1e-05)

    def step_at(c):
        return pl.ds(pl.multiple_of(c * step_rows, step_rows), step_rows)

    def pass_on(c):
        mid = sw.at[core, :, step_at(c)]
        return send(mid, mid, sw_s.at[c], sw_r.at[c], beside)

    def activate(c):
        for q in range(4):
            scale = norm[4 + q : 5 + q, :] * par[q, n_tap : n_tap + 1, :]
            x = (conv[q, step_at(c), :] - norm[q : q + 1, :]) * scale
            x = x + par[q, n_tap + 1 : n_tap + 2, :]
            lanes = slice((q % 2) * LANES, (q % 2 + 1) * LANES)
            sw[core, q // 2, step_at(c), lanes] = swish_gate(x, x).astype(BF16)
        pass_on(c).start()

    def home_rows(c):
        return pl.ds(pl.multiple_of(y * rows + c * step_rows, step_rows), step_rows)

    def give(c):
        return send(ob.at[step_at(c)], out.at[home_rows(c)], oy_s.at[c], oy_r.at[c], across)

    def project(c):
        pass_on(c).wait_recv()
        x = jnp.concatenate([sw[j % 2, j // 2, step_at(c), :] for j in range(4)], axis=1)
        ob[step_at(c), :] = jnp.dot(x, wd[oy], preferred_element_type=F32).astype(BF16)
        give(c).start()
        out[home_rows(c), :] = jnp.dot(x, wd[y], preferred_element_type=F32).astype(BF16)

    def ready():
        for h in range(2):
            down_keep(h).wait()
            down_beside(h).wait_recv()
        for key in shares:
            down_share(*key).wait_recv()
        for key in kept:
            down_share(*key).wait()

    def advance(c, carry):
        pl.when(c < STEPS)(lambda: activate(c))
        pl.when(c == 1)(ready)
        pl.when(c > 0)(lambda: project(c - 1))
        return carry

    lax.fori_loop(0, STEPS + 1, advance, 0)

    par_copy.wait_send()
    for half in (y, oy):
        for copy in halos(half):
            copy.wait_send()
    for k in range(2):
        for i in range(2):
            share(k, i).wait_send()
            relay(k, i).wait_send()
    down_cross.wait_send()
    for h in range(2):
        down_beside(h).wait_send()
    for key in shares:
        down_share(*key).wait_send()
    landed(stat.at[pl.ds(0, n_blocks - 1)], st_s)

    def drain(i, c):
        feat_beside(i).wait_send()
        feat_across(i).wait_send()
        feat_forward(i).wait_send()
        return c

    lax.fori_loop(0, PARTS, drain, 0)

    def finish(c, carry):
        pass_on(c).wait_send()
        give(c).wait()
        return carry

    lax.fori_loop(0, STEPS, finish, 0)


def body(
    n_tm,
    features, rec_start, rec_end, w_value, w_gate, depth_kernel, norm_gain, norm_shift, w_down,
):
    frames, width = features.shape
    depth = w_value.shape[0]
    rows = frames // 2
    dma = pltpu.SemaphoreType.DMA
    vmem = pl.BlockSpec(memory_space=pltpu.VMEM)
    n_blocks = 2 * n_tm
    return pl.pallas_call(
        functools.partial(kernel, n_tm),
        out_shape=jax.ShapeDtypeStruct((frames, width), BF16),
        in_specs=[pl.BlockSpec(memory_space=pltpu.HBM)] * 9,
        out_specs=vmem,
        scratch_shapes=[
            pltpu.VMEM((2, 2, depth, width), BF16),
            pltpu.VMEM((frames // LANES, LANES), jnp.int32),
            pltpu.VMEM((frames // LANES, LANES), jnp.int32),
            pltpu.VMEM(depth_kernel.shape, BF16),
            pltpu.VMEM((width,), BF16),
            pltpu.VMEM((width,), BF16),
            pltpu.VMEM((4, rows, width), BF16),
            pltpu.VMEM((2, 4 * width, width), BF16),
            pltpu.VMEM((width // GROUP, 4 * width), BF16),
            pltpu.VMEM((4, 16, LANES), F32),
            pltpu.VMEM((2, rows // LANES, LANES), F32),
            pltpu.VMEM((rows, LANES), F32),
            pltpu.VMEM((rows, LANES), F32),
            pltpu.VMEM((4, rows + 2 * PAD, LANES), F32),
            pltpu.VMEM((4, rows, LANES), F32),
            pltpu.VMEM((n_blocks, 8, LANES), F32),
            pltpu.VMEM((8, LANES), F32),
            pltpu.VMEM((2, 2, rows, width), BF16),
            pltpu.VMEM((rows, width), BF16),
            dma((12,)),
            dma((2,)), dma((2,)),
            dma((2, GROUP)), dma((2, GROUP)),
            dma, dma,
            dma((PARTS,)), dma((PARTS,)),
            dma((PARTS,)), dma((PARTS,)),
            dma((PARTS,)), dma((PARTS,)),
            dma((2, 2)), dma((2, 2)),
            dma, dma,
            dma((2,)), dma((2,)),
            dma((2, GROUP, 2)), dma((2, GROUP, 2)),
            dma, dma,
            dma((STEPS,)), dma((STEPS,)),
            dma((STEPS,)), dma((STEPS,)),
        ],
        compiler_params=pltpu.CompilerParams(
            collective_id=0, has_side_effects=True, vmem_limit_bytes=62 * 1024 * 1024
        ),
    )(
        features,
        rec_start.reshape(-1, LANES),
        rec_end.reshape(-1, LANES),
        w_value,
        w_gate,
        depth_kernel,
        norm_gain,
        norm_shift,
        w_down,
    )


def solution(mesh):
    in_specs = (
        P("tm", "chan"),
        P("tm"),
        P("tm"),
        P(None, "chan"),
        P(None, "chan"),
        P(None, "chan"),
        P("chan"),
        P("chan"),
        P("chan", None),
    )
    return jax.shard_map(
        functools.partial(body, mesh.shape["tm"]),
        mesh=mesh,
        in_specs=in_specs,
        out_specs=P("tm", "chan"),
        check_vma=False,
    )
```

```python
import functools

import jax
import jax.numpy as jnp
from jax import lax
from jax.experimental import pallas as pl
from jax.experimental.pallas import tpu as pltpu
from jax.sharding import PartitionSpec as P

F32, BF16 = jnp.float32, jnp.bfloat16
GROUP = 4
PARTS = 4
UNITS = 4
STEPS = 8
PAD = 8
BLOCK = 32
LANES = 128


def swish_gate(value, gate):
    return value * (0.5 * jnp.tanh(0.5 * gate) + 0.5)


def kernel(
    n_tm,
    feat, starts_in, ends_in, wv_in, wg_in, taps_in, gain_in, shift_in, wdown,
    out,
    w, starts, ends, taps, gain, shift,
    xg, wd, wdx, par, gap, back, fwd, glu, conv, stat, norm, sw, ob,
    loc, wy_s, wy_r, wf_s, wf_r, par_s, par_r, fc_s, fc_r, fy_s, fy_r, ff_s, ff_r,
    ha_s, ha_r, wx_s, wx_r, wb_s, wb_r, wd_s, wd_r, st_s, st_r, sw_s, sw_r, oy_s, oy_r,
):
    depth, width = wv_in.shape
    rows = feat.shape[0] // 2
    part, step_rows = rows // PARTS, rows // STEPS
    piece = depth // GROUP
    n_tap = taps.shape[0]
    reach = n_tap // 2
    n_blocks = 2 * n_tm
    total = n_blocks * rows

    t, chan = lax.axis_index("tm"), lax.axis_index("chan")
    y, core = chan // 2, chan % 2
    oy = 1 - y
    me = 2 * t + y
    across = (t, 2 * oy + core)
    beside = (t, 2 * y + 1 - core)
    group, g = t - t % GROUP, t % GROUP

    def at_block(b):
        return (b // 2, 2 * (b % 2) + core)

    def send(src, dst, s, r, to):
        return pltpu.make_async_remote_copy(
            src_ref=src, dst_ref=dst, send_sem=s, recv_sem=r,
            device_id=to, device_id_type=pl.DeviceIdType.MESH,
        )

    def landed(ref, sem):
        pltpu.make_async_copy(ref, ref, sem).wait()

    keep = pltpu.make_async_copy(
        feat.at[pl.ds(pl.multiple_of(y * rows, rows), rows)], xg.at[chan], loc.at[0]
    )
    loads = [
        pltpu.make_async_copy(src, dst, loc.at[3 + i])
        for i, (src, dst) in enumerate(
            (
                (starts_in, starts),
                (ends_in, ends),
                (taps_in, taps),
                (gain_in, gain),
                (shift_in, shift),
                (wv_in, w.at[y, 0]),
                (wg_in, w.at[y, 1]),
            )
        )
    ]
    for copy in loads:
        copy.start()
    keep.start()

    barrier = pltpu.get_barrier_semaphore()

    def greet(i, c):
        pl.semaphore_signal(
            barrier, inc=1, device_id=at_block((me + i) % n_blocks),
            device_id_type=pl.DeviceIdType.MESH,
        )
        return c

    lax.fori_loop(1, n_blocks, greet, 0)
    for i in range(GROUP):
        pl.semaphore_signal(
            barrier, inc=1, device_id=(group + (g + i) % GROUP, beside[1]),
            device_id_type=pl.DeviceIdType.MESH,
        )
    pl.semaphore_wait(barrier, n_blocks - 1 + GROUP)

    mine = pl.ds(pl.multiple_of(g * piece, piece), piece)
    cross = [
        send(mat.at[mine], w.at[y, k, mine], wy_s.at[k], wy_r.at[k], across)
        for k, mat in enumerate((wv_in, wg_in))
    ]
    cross[0].start()

    def own_rows(i):
        return pl.ds(pl.multiple_of(y * rows + i * part, part), part)

    def other_rows(i):
        return pl.ds(pl.multiple_of(oy * rows + i * part, part), part)

    def part_rows(i):
        return pl.ds(pl.multiple_of(i * part, part), part)

    def feat_beside(i):
        return send(
            feat.at[own_rows(i)], xg.at[chan, part_rows(i)], fc_s.at[i], fc_r.at[i], beside
        )

    def feat_across(i):
        return send(
            feat.at[other_rows(i)], xg.at[chan, part_rows(i)], fy_s.at[i], fy_r.at[i], across
        )

    def feat_forward(i):
        slot = 2 * oy + core
        return send(
            xg.at[slot, part_rows(i)], xg.at[slot, part_rows(i)], ff_s.at[i], ff_r.at[i], beside
        )

    for i in range(PARTS):
        feat_beside(i).start()

    cross[0].wait_send()
    cross[1].start()
    for copy in loads[:5]:
        copy.wait()
    gain_row = gain[...].astype(F32).reshape(1, width)
    shift_row = shift[...].astype(F32).reshape(1, width)
    for q in range(2):
        lanes = slice(q * LANES, (q + 1) * LANES)
        par[2 * y + q] = jnp.zeros(par.shape[1:], F32)
        par[2 * y + q, 0:n_tap, :] = taps[:, lanes].astype(F32)
        par[2 * y + q, n_tap : n_tap + 1, :] = gain_row[:, lanes]
        par[2 * y + q, n_tap + 1 : n_tap + 2, :] = shift_row[:, lanes]
    my_par = par.at[pl.ds(2 * y, 2)]
    par_copy = send(my_par, my_par, par_s, par_r, across)
    par_copy.start()

    groups = rows // LANES
    base = t * 2 * rows + y * rows
    span = pl.ds(pl.multiple_of(y * groups, groups), groups)
    frame = (
        base
        + lax.broadcasted_iota(jnp.int32, (groups, LANES), 0) * LANES
        + lax.broadcasted_iota(jnp.int32, (groups, LANES), 1)
    )
    before = jnp.minimum(frame - starts[span, :], reach).astype(F32)
    after = jnp.minimum(ends[span, :] - 1 - frame, reach).astype(F32)
    gap[0], gap[1] = before, after

    def spread(r, c):
        tile = pl.ds(pl.multiple_of(r * LANES, LANES), LANES)
        back[tile, :] = jnp.broadcast_to(gap[0, pl.ds(r, 1), :], (LANES, LANES)).T
        fwd[tile, :] = jnp.broadcast_to(gap[1, pl.ds(r, 1), :], (LANES, LANES)).T
        return c

    lax.fori_loop(0, groups, spread, 0)

    near = (g + 1 - 2 * (g % 2), (g + 2) % GROUP)

    def share(k, i):
        return send(
            w.at[oy, k, mine], w.at[oy, k, mine], wf_s.at[k, i], wf_r.at[k, i],
            (group + near[i], chan),
        )

    def relay(k, i):
        held = pl.ds(pl.multiple_of(near[i] * piece + i * (piece // 2), piece // 2), piece // 2)
        return send(
            w.at[oy, k, held], w.at[oy, k, held], wf_s.at[k, 2 + i], wf_r.at[k, 2 + i],
            (group + near[1 - i], chan),
        )

    for k in range(2):
        cross[k].wait_recv()
        for i in range(2):
            share(k, i).start()
        if k == 0:
            cross[1].wait_send()
            feat_across(0).start()
    for i in range(1, PARTS):
        feat_across(i).start()
    keep.wait()
    for copy in loads[5:]:
        copy.wait()
    for k in range(2):
        for i in range(2):
            share(k, i).wait_recv()
            relay(k, i).start()

    unit = rows // UNITS
    per_unit = PARTS // UNITS

    def gated(i, half):
        at = pl.ds(pl.multiple_of(i * unit, unit), unit)
        x = jnp.concatenate([xg[j, at, :] for j in range(4)], axis=1)
        value = jnp.dot(x, w[half, 0], preferred_element_type=F32)
        gate = jnp.dot(x, w[half, 1], preferred_element_type=F32)
        both = swish_gate(value, gate).astype(BF16).astype(F32)
        to = pl.ds(pl.multiple_of(PAD + i * unit, PAD), unit)
        glu[2 * half, to, :] = both[:, :LANES]
        glu[2 * half + 1, to, :] = both[:, LANES:]

    def arrive(i):
        feat_across(i).wait_recv()
        feat_forward(i).start()
        feat_beside(i).wait_recv()

    def halos(half):
        pair = pl.ds(2 * half, 2)
        return (
            send(
                glu.at[pair, pl.ds(rows, PAD)], glu.at[pair, pl.ds(0, PAD)],
                ha_s.at[half, 0], ha_r.at[half, 0], at_block((me + 1) % n_blocks),
            ),
            send(
                glu.at[pair, pl.ds(PAD, PAD)], glu.at[pair, pl.ds(rows + PAD, PAD)],
                ha_s.at[half, 1], ha_r.at[half, 1], at_block((me + n_blocks - 1) % n_blocks),
            ),
        )

    down_piece = width // GROUP
    cut = pl.ds(pl.multiple_of(g * down_piece, down_piece), down_piece)
    down_cross = send(wdown.at[cut], wdx, wx_s, wx_r, across)

    def down_cols(h, c):
        return pl.ds(pl.multiple_of((2 * h + c) * width, width), width)

    own_held = pl.ds(pl.multiple_of(chan * width, width), width)

    def down_beside(h):
        return send(
            wdown.at[:, down_cols(h, 1 - core)], wd.at[h, own_held], wb_s.at[h], wb_r.at[h], beside
        )

    def down_keep(h):
        return pltpu.make_async_copy(
            wdown.at[:, down_cols(h, core)], wd.at[h, own_held], loc.at[1 + h]
        )

    def down_share(o, i, h):
        to_core = (core, 1 - core)[o]
        held = pl.ds(
            pl.multiple_of(across[1] * width + g * down_piece, down_piece), down_piece
        )
        src, dst = wdx.at[:, down_cols(h, to_core)], wd.at[h, held]
        if o == 0 and i == 0:
            return pltpu.make_async_copy(src, dst, loc.at[10 + h])
        to = (group + (g + i) % GROUP, 2 * y + to_core)
        return send(src, dst, wd_s.at[o, i, h], wd_r.at[o, i, h], to)

    shares = [
        (o, i, h) for i in (1, 2, 3, 0) for o in range(2) for h in range(2) if (o, i) != (0, 0)
    ]
    kept = [(0, 0, h) for h in range(2)]

    def inner(b, c):
        at = pl.multiple_of(b * BLOCK, BLOCK)
        room_back, room_fwd = back[pl.ds(at, BLOCK), :], fwd[pl.ds(at, BLOCK), :]
        accs = [jnp.zeros((BLOCK, LANES), F32)] * 4
        for k in range(n_tap):
            d = k - reach
            usable = room_back >= float(-d) if d < 0 else room_fwd >= float(d)
            for q in range(4):
                term = glu[q, pl.ds(at + (PAD + d), BLOCK), :] * par[q, k : k + 1, :]
                accs[q] = accs[q] + (term if d == 0 else jnp.where(usable, term, 0.0))
        for q in range(4):
            conv[q, pl.ds(at, BLOCK), :] = accs[q]
        return c

    n_inner = rows // BLOCK
    per_block = unit // BLOCK

    def settle(i, c):
        @pl.when(i < UNITS)
        def _():
            lax.fori_loop(i * per_unit, (i + 1) * per_unit, lambda n, c: arrive(n) or c, 0)

        @pl.when(i == UNITS - 2)
        def _():
            down_cross.start()

        @pl.when(i == 1)
        def _():
            for k in range(2):
                for n in range(2):
                    relay(k, n).wait_recv()
            par_copy.wait_recv()
            for h in range(2):
                down_keep(h).start()
                down_beside(h).start()

        @pl.when(i > 0)
        def _():
            u = i - 1
            gated(u, oy)

            @pl.when(u == UNITS - 1)
            def _():
                for half in (y, oy):
                    for copy in halos(half):
                        copy.start()

            low = jnp.where(u == 0, 1, u * per_block - 1)
            lax.fori_loop(low, (u + 1) * per_block - 1, inner, 0)

        @pl.when(i < UNITS)
        def _():
            lax.fori_loop(
                i * per_unit, (i + 1) * per_unit, lambda n, c: feat_forward(n).wait_recv() or c, 0
            )
            gated(i, y)

        @pl.when(i == UNITS - 1)
        def _():
            down_cross.wait_recv()
            for key in shares + kept:
                down_share(*key).start()

        return c

    lax.fori_loop(0, UNITS + 1, settle, 0)
    for half in (y, oy):
        for copy in halos(half):
            copy.wait_recv()
    lax.fori_loop(0, 2, lambda n, c: inner(n * (n_inner - 1), c), 0)

    def gather(q, c):
        block = conv[q]
        total_q = jnp.sum(block, axis=0, keepdims=True)
        off = block - total_q * (1.0 / rows)
        stat[me, pl.ds(q, 1), :] = total_q
        stat[me, pl.ds(4 + q, 1), :] = jnp.sum(off * off, axis=0, keepdims=True)
        return c

    lax.fori_loop(0, 4, gather, 0)

    def tell(i, c):
        send(stat.at[me], stat.at[me], st_s, st_r, at_block((me + i) % n_blocks)).start()
        return c

    lax.fori_loop(1, n_blocks, tell, 0)
    landed(stat.at[pl.ds(0, n_blocks - 1)], st_r)
    sums, squares = stat[:, 0:4, :], stat[:, 4:8, :]
    mean = jnp.sum(sums, axis=0) * (1.0 / total)
    drift = sums * (1.0 / rows) - mean[None]
    var = jnp.sum(squares + float(rows) * (drift * drift), axis=0) * (1.0 / total)
    norm[0:4, :] = mean
    norm[4:8, :] = 1.0 / jnp.sqrt(var + 1e-05)

    def step_at(c):
        return pl.ds(pl.multiple_of(c * step_rows, step_rows), step_rows)

    def pass_on(c):
        mid = sw.at[core, :, step_at(c)]
        return send(mid, mid, sw_s.at[c], sw_r.at[c], beside)

    def activate(c):
        for q in range(4):
            scale = norm[4 + q : 5 + q, :] * par[q, n_tap : n_tap + 1, :]
            x = (conv[q, step_at(c), :] - norm[q : q + 1, :]) * scale
            x = x + par[q, n_tap + 1 : n_tap + 2, :]
            lanes = slice((q % 2) * LANES, (q % 2 + 1) * LANES)
            sw[core, q // 2, step_at(c), lanes] = swish_gate(x, x).astype(BF16)
        pass_on(c).start()

    def home_rows(c):
        return pl.ds(pl.multiple_of(y * rows + c * step_rows, step_rows), step_rows)

    def give(c):
        return send(ob.at[step_at(c)], out.at[home_rows(c)], oy_s.at[c], oy_r.at[c], across)

    def project(c):
        pass_on(c).wait_recv()
        x = jnp.concatenate([sw[j % 2, j // 2, step_at(c), :] for j in range(4)], axis=1)
        ob[step_at(c), :] = jnp.dot(x, wd[oy], preferred_element_type=F32).astype(BF16)
        give(c).start()
        out[home_rows(c), :] = jnp.dot(x, wd[y], preferred_element_type=F32).astype(BF16)

    def ready():
        for h in range(2):
            down_keep(h).wait()
            down_beside(h).wait_recv()
        for key in shares:
            down_share(*key).wait_recv()
        for key in kept:
            down_share(*key).wait()

    def advance(c, carry):
        pl.when(c < STEPS)(lambda: activate(c))
        pl.when(c == 1)(ready)
        pl.when(c > 0)(lambda: project(c - 1))
        return carry

    lax.fori_loop(0, STEPS + 1, advance, 0)

    par_copy.wait_send()
    for half in (y, oy):
        for copy in halos(half):
            copy.wait_send()
    for k in range(2):
        for i in range(2):
            share(k, i).wait_send()
            relay(k, i).wait_send()
    down_cross.wait_send()
    for h in range(2):
        down_beside(h).wait_send()
    for key in shares:
        down_share(*key).wait_send()
    landed(stat.at[pl.ds(0, n_blocks - 1)], st_s)

    def drain(i, c):
        feat_beside(i).wait_send()
        feat_across(i).wait_send()
        feat_forward(i).wait_send()
        return c

    lax.fori_loop(0, PARTS, drain, 0)

    def finish(c, carry):
        pass_on(c).wait_send()
        give(c).wait()
        return carry

    lax.fori_loop(0, STEPS, finish, 0)


def body(
    n_tm,
    features, rec_start, rec_end, w_value, w_gate, depth_kernel, norm_gain, norm_shift, w_down,
):
    frames, width = features.shape
    depth = w_value.shape[0]
    rows = frames // 2
    dma = pltpu.SemaphoreType.DMA
    vmem = pl.BlockSpec(memory_space=pltpu.VMEM)
    n_blocks = 2 * n_tm
    return pl.pallas_call(
        functools.partial(kernel, n_tm),
        out_shape=jax.ShapeDtypeStruct((frames, width), BF16),
        in_specs=[pl.BlockSpec(memory_space=pltpu.HBM)] * 9,
        out_specs=vmem,
        scratch_shapes=[
            pltpu.VMEM((2, 2, depth, width), BF16),
            pltpu.VMEM((frames // LANES, LANES), jnp.int32),
            pltpu.VMEM((frames // LANES, LANES), jnp.int32),
            pltpu.VMEM(depth_kernel.shape, BF16),
            pltpu.VMEM((width,), BF16),
            pltpu.VMEM((width,), BF16),
            pltpu.VMEM((4, rows, width), BF16),
            pltpu.VMEM((2, 4 * width, width), BF16),
            pltpu.VMEM((width // GROUP, 4 * width), BF16),
            pltpu.VMEM((4, 16, LANES), F32),
            pltpu.VMEM((2, rows // LANES, LANES), F32),
            pltpu.VMEM((rows, LANES), F32),
            pltpu.VMEM((rows, LANES), F32),
            pltpu.VMEM((4, rows + 2 * PAD, LANES), F32),
            pltpu.VMEM((4, rows, LANES), F32),
            pltpu.VMEM((n_blocks, 8, LANES), F32),
            pltpu.VMEM((8, LANES), F32),
            pltpu.VMEM((2, 2, rows, width), BF16),
            pltpu.VMEM((rows, width), BF16),
            dma((12,)),
            dma((2,)), dma((2,)),
            dma((2, GROUP)), dma((2, GROUP)),
            dma, dma,
            dma((PARTS,)), dma((PARTS,)),
            dma((PARTS,)), dma((PARTS,)),
            dma((PARTS,)), dma((PARTS,)),
            dma((2, 2)), dma((2, 2)),
            dma, dma,
            dma((2,)), dma((2,)),
            dma((2, GROUP, 2)), dma((2, GROUP, 2)),
            dma, dma,
            dma((STEPS,)), dma((STEPS,)),
            dma((STEPS,)), dma((STEPS,)),
        ],
        compiler_params=pltpu.CompilerParams(
            collective_id=0, has_side_effects=True, vmem_limit_bytes=62 * 1024 * 1024
        ),
    )(
        features,
        rec_start.reshape(-1, LANES),
        rec_end.reshape(-1, LANES),
        w_value,
        w_gate,
        depth_kernel,
        norm_gain,
        norm_shift,
        w_down,
    )


def solution(mesh):
    in_specs = (
        P("tm", "chan"),
        P("tm"),
        P("tm"),
        P(None, "chan"),
        P(None, "chan"),
        P(None, "chan"),
        P("chan"),
        P("chan"),
        P("chan", None),
    )
    return jax.shard_map(
        functools.partial(body, mesh.shape["tm"]),
        mesh=mesh,
        in_specs=in_specs,
        out_specs=P("tm", "chan"),
        check_vma=False,
    )
```

```python
import functools

import jax
import jax.numpy as jnp
from jax import lax
from jax.experimental import pallas as pl
from jax.experimental.pallas import tpu as pltpu
from jax.sharding import PartitionSpec as P

F32, BF16 = jnp.float32, jnp.bfloat16
GROUP = 4
PARTS = 4
UNITS = 2
STEPS = 4
PAD = 8
BLOCK = 64
LANES = 128


def swish_gate(value, gate):
    return value * (0.5 * jnp.tanh(0.5 * gate) + 0.5)


def kernel(
    n_tm,
    feat, starts_in, ends_in, wv_in, wg_in, taps_in, gain_in, shift_in, wdown,
    out,
    w, starts, ends, taps, gain, shift,
    xg, wd, wdx, par, gap, back, fwd, glu, conv, stat, norm, sw, ob,
    loc, wy_s, wy_r, wf_s, wf_r, par_s, par_r, fc_s, fc_r, fy_s, fy_r, ff_s, ff_r,
    ha_s, ha_r, wx_s, wx_r, wb_s, wb_r, wd_s, wd_r, st_s, st_r, sw_s, sw_r, oy_s, oy_r,
):
    depth, width = wv_in.shape
    rows = feat.shape[0] // 2
    part, step_rows = rows // PARTS, rows // STEPS
    piece = depth // GROUP
    n_tap = taps.shape[0]
    reach = n_tap // 2
    n_blocks = 2 * n_tm
    total = n_blocks * rows

    t, chan = lax.axis_index("tm"), lax.axis_index("chan")
    y, core = chan // 2, chan % 2
    oy = 1 - y
    me = 2 * t + y
    across = (t, 2 * oy + core)
    beside = (t, 2 * y + 1 - core)
    group, g = t - t % GROUP, t % GROUP

    def at_block(b):
        return (b // 2, 2 * (b % 2) + core)

    def send(src, dst, s, r, to):
        return pltpu.make_async_remote_copy(
            src_ref=src, dst_ref=dst, send_sem=s, recv_sem=r,
            device_id=to, device_id_type=pl.DeviceIdType.MESH,
        )

    def landed(ref, sem):
        pltpu.make_async_copy(ref, ref, sem).wait()

    keep = pltpu.make_async_copy(
        feat.at[pl.ds(pl.multiple_of(y * rows, rows), rows)], xg.at[chan], loc.at[0]
    )
    loads = [
        pltpu.make_async_copy(src, dst, loc.at[3 + i])
        for i, (src, dst) in enumerate(
            (
                (starts_in, starts),
                (ends_in, ends),
                (taps_in, taps),
                (gain_in, gain),
                (shift_in, shift),
                (wv_in, w.at[y, 0]),
                (wg_in, w.at[y, 1]),
            )
        )
    ]
    for copy in loads:
        copy.start()
    keep.start()

    barrier = pltpu.get_barrier_semaphore()

    def greet(i, c):
        pl.semaphore_signal(
            barrier, inc=1, device_id=at_block((me + i) % n_blocks),
            device_id_type=pl.DeviceIdType.MESH,
        )
        return c

    lax.fori_loop(1, n_blocks, greet, 0)
    for i in range(GROUP):
        pl.semaphore_signal(
            barrier, inc=1, device_id=(group + (g + i) % GROUP, beside[1]),
            device_id_type=pl.DeviceIdType.MESH,
        )
    pl.semaphore_wait(barrier, n_blocks - 1 + GROUP)

    mine = pl.ds(pl.multiple_of(g * piece, piece), piece)
    cross = [
        send(mat.at[mine], w.at[y, k, mine], wy_s.at[k], wy_r.at[k], across)
        for k, mat in enumerate((wv_in, wg_in))
    ]
    cross[0].start()

    def own_rows(i):
        return pl.ds(pl.multiple_of(y * rows + i * part, part), part)

    def other_rows(i):
        return pl.ds(pl.multiple_of(oy * rows + i * part, part), part)

    def part_rows(i):
        return pl.ds(pl.multiple_of(i * part, part), part)

    def feat_beside(i):
        return send(
            feat.at[own_rows(i)], xg.at[chan, part_rows(i)], fc_s.at[i], fc_r.at[i], beside
        )

    def feat_across(i):
        return send(
            feat.at[other_rows(i)], xg.at[chan, part_rows(i)], fy_s.at[i], fy_r.at[i], across
        )

    def feat_forward(i):
        slot = 2 * oy + core
        return send(
            xg.at[slot, part_rows(i)], xg.at[slot, part_rows(i)], ff_s.at[i], ff_r.at[i], beside
        )

    for i in range(PARTS):
        feat_beside(i).start()

    cross[0].wait_send()
    cross[1].start()
    for copy in loads[:5]:
        copy.wait()
    gain_row = gain[...].astype(F32).reshape(1, width)
    shift_row = shift[...].astype(F32).reshape(1, width)
    for q in range(2):
        lanes = slice(q * LANES, (q + 1) * LANES)
        par[2 * y + q] = jnp.zeros(par.shape[1:], F32)
        par[2 * y + q, 0:n_tap, :] = taps[:, lanes].astype(F32)
        par[2 * y + q, n_tap : n_tap + 1, :] = gain_row[:, lanes]
        par[2 * y + q, n_tap + 1 : n_tap + 2, :] = shift_row[:, lanes]
    my_par = par.at[pl.ds(2 * y, 2)]
    par_copy = send(my_par, my_par, par_s, par_r, across)
    par_copy.start()

    groups = rows // LANES
    base = t * 2 * rows + y * rows
    span = pl.ds(pl.multiple_of(y * groups, groups), groups)
    frame = (
        base
        + lax.broadcasted_iota(jnp.int32, (groups, LANES), 0) * LANES
        + lax.broadcasted_iota(jnp.int32, (groups, LANES), 1)
    )
    before = jnp.minimum(frame - starts[span, :], reach).astype(F32)
    after = jnp.minimum(ends[span, :] - 1 - frame, reach).astype(F32)
    gap[0], gap[1] = before, after

    def spread(r, c):
        tile = pl.ds(pl.multiple_of(r * LANES, LANES), LANES)
        back[tile, :] = jnp.broadcast_to(gap[0, pl.ds(r, 1), :], (LANES, LANES)).T
        fwd[tile, :] = jnp.broadcast_to(gap[1, pl.ds(r, 1), :], (LANES, LANES)).T
        return c

    lax.fori_loop(0, groups, spread, 0)

    near = (g + 1 - 2 * (g % 2), (g + 2) % GROUP)

    def share(k, i):
        return send(
            w.at[oy, k, mine], w.at[oy, k, mine], wf_s.at[k, i], wf_r.at[k, i],
            (group + near[i], chan),
        )

    def relay(k, i):
        held = pl.ds(pl.multiple_of(near[i] * piece + i * (piece // 2), piece // 2), piece // 2)
        return send(
            w.at[oy, k, held], w.at[oy, k, held], wf_s.at[k, 2 + i], wf_r.at[k, 2 + i],
            (group + near[1 - i], chan),
        )

    for k in range(2):
        cross[k].wait_recv()
        for i in range(2):
            share(k, i).start()
        if k == 0:
            cross[1].wait_send()
            feat_across(0).start()
    for i in range(1, PARTS):
        feat_across(i).start()
    keep.wait()
    for copy in loads[5:]:
        copy.wait()
    for k in range(2):
        for i in range(2):
            share(k, i).wait_recv()
            relay(k, i).start()

    unit = rows // UNITS
    per_unit = PARTS // UNITS

    def gated(i, half):
        at = pl.ds(pl.multiple_of(i * unit, unit), unit)
        x = jnp.concatenate([xg[j, at, :] for j in range(4)], axis=1)
        value = jnp.dot(x, w[half, 0], preferred_element_type=F32)
        gate = jnp.dot(x, w[half, 1], preferred_element_type=F32)
        both = swish_gate(value, gate).astype(BF16).astype(F32)
        to = pl.ds(pl.multiple_of(PAD + i * unit, PAD), unit)
        glu[2 * half, to, :] = both[:, :LANES]
        glu[2 * half + 1, to, :] = both[:, LANES:]

    def arrive(i):
        feat_across(i).wait_recv()
        feat_forward(i).start()
        feat_beside(i).wait_recv()

    def halos(half):
        pair = pl.ds(2 * half, 2)
        return (
            send(
                glu.at[pair, pl.ds(rows, PAD)], glu.at[pair, pl.ds(0, PAD)],
                ha_s.at[half, 0], ha_r.at[half, 0], at_block((me + 1) % n_blocks),
            ),
            send(
                glu.at[pair, pl.ds(PAD, PAD)], glu.at[pair, pl.ds(rows + PAD, PAD)],
                ha_s.at[half, 1], ha_r.at[half, 1], at_block((me + n_blocks - 1) % n_blocks),
            ),
        )

    down_piece = width // GROUP
    cut = pl.ds(pl.multiple_of(g * down_piece, down_piece), down_piece)
    down_cross = send(wdown.at[cut], wdx, wx_s, wx_r, across)

    def down_cols(h, c):
        return pl.ds(pl.multiple_of((2 * h + c) * width, width), width)

    own_held = pl.ds(pl.multiple_of(chan * width, width), width)

    def down_beside(h):
        return send(
            wdown.at[:, down_cols(h, 1 - core)], wd.at[h, own_held], wb_s.at[h], wb_r.at[h], beside
        )

    def down_keep(h):
        return pltpu.make_async_copy(
            wdown.at[:, down_cols(h, core)], wd.at[h, own_held], loc.at[1 + h]
        )

    def down_share(o, i, h):
        to_core = (core, 1 - core)[o]
        held = pl.ds(
            pl.multiple_of(across[1] * width + g * down_piece, down_piece), down_piece
        )
        src, dst = wdx.at[:, down_cols(h, to_core)], wd.at[h, held]
        if o == 0 and i == 0:
            return pltpu.make_async_copy(src, dst, loc.at[10 + h])
        to = (group + (g + i) % GROUP, 2 * y + to_core)
        return send(src, dst, wd_s.at[o, i, h], wd_r.at[o, i, h], to)

    shares = [
        (o, i, h) for i in (1, 2, 3, 0) for o in range(2) for h in range(2) if (o, i) != (0, 0)
    ]
    kept = [(0, 0, h) for h in range(2)]

    def convolve(q, b):
        at = pl.multiple_of(b * BLOCK, BLOCK)
        room_back, room_fwd = back[pl.ds(at, BLOCK), :], fwd[pl.ds(at, BLOCK), :]
        acc = jnp.zeros((BLOCK, LANES), F32)
        for k in range(n_tap):
            d = k - reach
            term = glu[q, pl.ds(at + (PAD + d), BLOCK), :] * par[q, k : k + 1, :]
            if d < 0:
                term = jnp.where(room_back >= float(-d), term, 0.0)
            elif d > 0:
                term = jnp.where(room_fwd >= float(d), term, 0.0)
            acc = acc + term
        conv[q, pl.ds(at, BLOCK), :] = acc

    n_inner = rows // BLOCK
    per_block = unit // BLOCK

    def inner(b, c):
        def one(q, c):
            convolve(q, b)
            return c

        return lax.fori_loop(0, 4, one, c)

    def settle(i, c):
        lax.fori_loop(i * per_unit, (i + 1) * per_unit, lambda n, c: arrive(n) or c, 0)

        @pl.when(i == UNITS - 1)
        def _():
            down_cross.start()

        lax.fori_loop(
            i * per_unit, (i + 1) * per_unit, lambda n, c: feat_forward(n).wait_recv() or c, 0
        )

        def product(j, c):
            @pl.when((i == 0) & (j == 1))
            def _():
                for k in range(2):
                    for n in range(2):
                        relay(k, n).wait_recv()

            gated(i, (y + j) % 2)
            return c

        lax.fori_loop(0, 2, product, 0)

        @pl.when(i == 0)
        def _():
            par_copy.wait_recv()
            for h in range(2):
                down_keep(h).start()
                down_beside(h).start()

        @pl.when(i == UNITS - 1)
        def _():
            for half in (y, oy):
                for copy in halos(half):
                    copy.start()

        low = jnp.where(i == 0, 1, i * per_block - 1)
        lax.fori_loop(low, (i + 1) * per_block - 1, inner, 0)
        return c

    lax.fori_loop(0, UNITS, settle, 0)
    down_cross.wait_recv()
    for key in shares + kept:
        down_share(*key).start()
    for half in (y, oy):
        for copy in halos(half):
            copy.wait_recv()
    lax.fori_loop(0, 2, lambda n, c: inner(n * (n_inner - 1), c), 0)

    def gather(q, c):
        block = conv[q]
        total_q = jnp.sum(block, axis=0, keepdims=True)
        off = block - total_q * (1.0 / rows)
        stat[me, pl.ds(q, 1), :] = total_q
        stat[me, pl.ds(4 + q, 1), :] = jnp.sum(off * off, axis=0, keepdims=True)
        return c

    lax.fori_loop(0, 4, gather, 0)

    def tell(i, c):
        send(stat.at[me], stat.at[me], st_s, st_r, at_block((me + i) % n_blocks)).start()
        return c

    lax.fori_loop(1, n_blocks, tell, 0)
    landed(stat.at[pl.ds(0, n_blocks - 1)], st_r)
    sums, squares = stat[:, 0:4, :], stat[:, 4:8, :]
    mean = jnp.sum(sums, axis=0) * (1.0 / total)
    drift = sums * (1.0 / rows) - mean[None]
    var = jnp.sum(squares + float(rows) * (drift * drift), axis=0) * (1.0 / total)
    norm[0:4, :] = mean
    norm[4:8, :] = 1.0 / jnp.sqrt(var + 1e-05)

    def step_at(c):
        return pl.ds(pl.multiple_of(c * step_rows, step_rows), step_rows)

    def pass_on(c):
        mid = sw.at[core, :, step_at(c)]
        return send(mid, mid, sw_s.at[c], sw_r.at[c], beside)

    def activate(c):
        for q in range(4):
            scale = norm[4 + q : 5 + q, :] * par[q, n_tap : n_tap + 1, :]
            x = (conv[q, step_at(c), :] - norm[q : q + 1, :]) * scale
            x = x + par[q, n_tap + 1 : n_tap + 2, :]
            lanes = slice((q % 2) * LANES, (q % 2 + 1) * LANES)
            sw[core, q // 2, step_at(c), lanes] = swish_gate(x, x).astype(BF16)
        pass_on(c).start()

    def home_rows(c):
        return pl.ds(pl.multiple_of(y * rows + c * step_rows, step_rows), step_rows)

    def give(c):
        return send(ob.at[step_at(c)], out.at[home_rows(c)], oy_s.at[c], oy_r.at[c], across)

    def mixed(c, half):
        x = jnp.concatenate([sw[j % 2, j // 2, step_at(c), :] for j in range(4)], axis=1)
        return jnp.dot(x, wd[half], preferred_element_type=F32).astype(BF16)

    def project(c):
        pass_on(c).wait_recv()
        ob[step_at(c), :] = mixed(c, oy)
        give(c).start()

    def stay(c, carry):
        out[home_rows(c), :] = mixed(c, y)
        return carry

    def ready():
        for h in range(2):
            down_keep(h).wait()
            down_beside(h).wait_recv()
        for key in shares:
            down_share(*key).wait_recv()
        for key in kept:
            down_share(*key).wait()

    def advance(c, carry):
        pl.when(c < STEPS)(lambda: activate(c))
        pl.when(c == 1)(ready)
        pl.when(c > 0)(lambda: project(c - 1))
        return carry

    lax.fori_loop(0, STEPS + 1, advance, 0)
    lax.fori_loop(0, STEPS, stay, 0)

    par_copy.wait_send()
    for half in (y, oy):
        for copy in halos(half):
            copy.wait_send()
    for k in range(2):
        for i in range(2):
            share(k, i).wait_send()
            relay(k, i).wait_send()
    down_cross.wait_send()
    for h in range(2):
        down_beside(h).wait_send()
    for key in shares:
        down_share(*key).wait_send()
    landed(stat.at[pl.ds(0, n_blocks - 1)], st_s)

    def drain(i, c):
        feat_beside(i).wait_send()
        feat_across(i).wait_send()
        feat_forward(i).wait_send()
        return c

    lax.fori_loop(0, PARTS, drain, 0)

    def finish(c, carry):
        pass_on(c).wait_send()
        give(c).wait()
        return carry

    lax.fori_loop(0, STEPS, finish, 0)


def body(
    n_tm,
    features, rec_start, rec_end, w_value, w_gate, depth_kernel, norm_gain, norm_shift, w_down,
):
    frames, width = features.shape
    depth = w_value.shape[0]
    rows = frames // 2
    dma = pltpu.SemaphoreType.DMA
    vmem = pl.BlockSpec(memory_space=pltpu.VMEM)
    n_blocks = 2 * n_tm
    return pl.pallas_call(
        functools.partial(kernel, n_tm),
        out_shape=jax.ShapeDtypeStruct((frames, width), BF16),
        in_specs=[pl.BlockSpec(memory_space=pltpu.HBM)] * 9,
        out_specs=vmem,
        scratch_shapes=[
            pltpu.VMEM((2, 2, depth, width), BF16),
            pltpu.VMEM((frames // LANES, LANES), jnp.int32),
            pltpu.VMEM((frames // LANES, LANES), jnp.int32),
            pltpu.VMEM(depth_kernel.shape, BF16),
            pltpu.VMEM((width,), BF16),
            pltpu.VMEM((width,), BF16),
            pltpu.VMEM((4, rows, width), BF16),
            pltpu.VMEM((2, 4 * width, width), BF16),
            pltpu.VMEM((width // GROUP, 4 * width), BF16),
            pltpu.VMEM((4, 16, LANES), F32),
            pltpu.VMEM((2, rows // LANES, LANES), F32),
            pltpu.VMEM((rows, LANES), F32),
            pltpu.VMEM((rows, LANES), F32),
            pltpu.VMEM((4, rows + 2 * PAD, LANES), F32),
            pltpu.VMEM((4, rows, LANES), F32),
            pltpu.VMEM((n_blocks, 8, LANES), F32),
            pltpu.VMEM((8, LANES), F32),
            pltpu.VMEM((2, 2, rows, width), BF16),
            pltpu.VMEM((rows, width), BF16),
            dma((12,)),
            dma((2,)), dma((2,)),
            dma((2, GROUP)), dma((2, GROUP)),
            dma, dma,
            dma((PARTS,)), dma((PARTS,)),
            dma((PARTS,)), dma((PARTS,)),
            dma((PARTS,)), dma((PARTS,)),
            dma((2, 2)), dma((2, 2)),
            dma, dma,
            dma((2,)), dma((2,)),
            dma((2, GROUP, 2)), dma((2, GROUP, 2)),
            dma, dma,
            dma((STEPS,)), dma((STEPS,)),
            dma((STEPS,)), dma((STEPS,)),
        ],
        compiler_params=pltpu.CompilerParams(
            collective_id=0, has_side_effects=True, vmem_limit_bytes=62 * 1024 * 1024
        ),
    )(
        features,
        rec_start.reshape(-1, LANES),
        rec_end.reshape(-1, LANES),
        w_value,
        w_gate,
        depth_kernel,
        norm_gain,
        norm_shift,
        w_down,
    )


def solution(mesh):
    in_specs = (
        P("tm", "chan"),
        P("tm"),
        P("tm"),
        P(None, "chan"),
        P(None, "chan"),
        P(None, "chan"),
        P("chan"),
        P("chan"),
        P("chan", None),
    )
    return jax.shard_map(
        functools.partial(body, mesh.shape["tm"]),
        mesh=mesh,
        in_specs=in_specs,
        out_specs=P("tm", "chan"),
        check_vma=False,
    )
```
